32 devices in a mesh: batch: 8 (over y, x, core), mp: 4 (over z).
Axes of the slice: x: 2, y: 2, z: 4, core: 2. Of those that a mesh axis runs over, the one named last changes fastest.
Arguments:
- residual: bfloat16 [8, 64, 8192], P('batch', None, 'mp'), may hold values from -6 to 6
- query_states: bfloat16 [8, 64, 4096], P('batch', None, 'mp')
- key_states: bfloat16 [8, 64, 512], P('batch')
- value_states: bfloat16 [8, 64, 512], P('batch'), may hold values from -6 to 6
- prompt_perm: int32 [8], replicated, may hold values from 0 to 7, each once
- ablated_heads: int32 [8], replicated, may hold values from 0 to 31, as said below
- out_weight: bfloat16 [4096, 8192], P('batch', 'mp'), may hold values from -0.09375 to 0.09375
- rms_gain: float32 [8192], P('mp'), may hold values from 0.1 to 1.9
- gate_weight: bfloat16 [8192, 14336], P('mp', 'batch'), may hold values from -0.0625 to 0.0625
- up_weight: bfloat16 [8192, 14336], P('mp', 'batch'), may hold values from -0.0625 to 0.0625
- down_weight: bfloat16 [14336, 8192], P('batch', 'mp'), may hold values from -0.046875 to 0.046875
Outputs:
- attn_out: bfloat16 [8, 64, 8192], P('batch', None, 'mp')
- mlp_out: bfloat16 [8, 64, 8192], P('batch', None, 'mp')
The draws below stay inside these ranges and needn't reach their ends.
Inputs may be any that keep to these rules, and one draw needn't show every extreme that they name: `prompt_perm`: each prompt index appears exactly once. `ablated_heads`: 8 different head indices in any order, one of them 32 - 1.
All inputs are finite; a program needn't handle non-finite values.
Results may differ from the reference program's by a relative error of at most 0.035.
Values may be sent and summed in bfloat16 or wider, within the bound.
A program may use at most 128 MiB of HBM per device.

```python
import math
import jax
import jax.numpy as jnp
from jax import lax

D = 8192
HEADS = 32
KV = 4
HD = 128
FF = 14336
ABLATED = 8
SEQ = 64
PROMPTS = 8
N_BATCH = 8


def key_table(key):
    return jax.random.normal(jax.random.fold_in(key, 11), (PROMPTS, SEQ, KV * HD), jnp.float32)


def draw_key_states(key, part):
    return key_table(key).astype(jnp.bfloat16)


def draw_query_states(key, part):
    base = jax.random.normal(jax.random.fold_in(key, 23), (PROMPTS, SEQ, HEADS * HD), jnp.float32)
    return base.astype(jnp.bfloat16)


def draw_ablated_heads(key, part):
    others = jax.random.permutation(jax.random.fold_in(key, 37), HEADS - 1)[:ABLATED - 1].astype(jnp.int32)
    listed = jnp.concatenate([others, jnp.full((1,), HEADS - 1, jnp.int32)])
    order = jax.random.permutation(jax.random.fold_in(key, 41), ABLATED)
    return jnp.take(listed, order).astype(jnp.int32)


def block_levels(stream_key, extent, cuts, low, high):
    level, own = 1.0, jax.random.fold_in(stream_key, 6)
    for axis_at, shards_of in cuts:
        heights = jnp.exp(jax.random.uniform(jax.random.fold_in(own, axis_at), (shards_of,), jnp.float32, low / len(cuts), high / len(cuts)))
        level = level * jnp.repeat(heights, extent[axis_at] // shards_of).reshape([-1 if axis == axis_at else 1 for axis in range(len(extent))])
    return level


def normal_values(rng, shape, scale, most, shards=(), held_as=jnp.bfloat16):
    factor_of = block_levels(rng, shape, shards, -0.22, 0.18) if shards else 1.0
    result = jax.random.normal(rng, shape, jnp.float32) * scale * factor_of
    return jnp.minimum(jnp.maximum(result, -most), most).astype(held_as)


def setup_inputs(seed: int = 0) -> dict:
    seeds = jax.random.split(jax.random.key(seed), 12)
    residual = normal_values(seeds[0], (PROMPTS, SEQ, D), 1.0, 6.0, ((0, 8), (2, 4)))
    query_states = draw_query_states(jax.random.fold_in(seeds[11], 71), 0)
    key_states = draw_key_states(jax.random.fold_in(seeds[11], 71), 0)
    value_states = normal_values(seeds[3], (PROMPTS, SEQ, KV * HD), 1.0, 6.0, ((0, 8),))
    prompt_perm = jax.random.permutation(seeds[4], PROMPTS).astype(jnp.int32)
    ablated_heads = draw_ablated_heads(jax.random.fold_in(seeds[11], 71), 0)
    out_weight = normal_values(seeds[6], (HEADS * HD, D), (HEADS * HD) ** -0.5, 0.09375, ((0, 8), (1, 4)))
    rms_gain = jnp.clip(1.0 + 0.18 * jax.random.normal(seeds[7], (D,), jnp.float32), 0.1, 1.9)
    gate_weight = normal_values(seeds[8], (D, FF), D ** -0.5, 0.0625, ((0, 4), (1, 8)))
    up_weight = normal_values(seeds[9], (D, FF), D ** -0.5, 0.0625, ((0, 4), (1, 8)))
    down_weight = normal_values(seeds[10], (FF, D), FF ** -0.5, 0.046875, ((0, 8), (1, 4)))
    return dict(residual=residual, query_states=query_states, key_states=key_states, value_states=value_states, prompt_perm=prompt_perm, ablated_heads=ablated_heads, out_weight=out_weight, rms_gain=rms_gain, gate_weight=gate_weight, up_weight=up_weight, down_weight=down_weight)


def attend_prompt(triple):
    query_rows, key_rows, value_rows = triple
    grouped = query_rows.astype(jnp.float32).reshape(SEQ, KV, HEADS // KV, HD)
    key_float = key_rows.astype(jnp.float32).reshape(SEQ, KV, HD)
    value_float = value_rows.astype(jnp.float32).reshape(SEQ, KV, HD)
    scores = jnp.einsum('skgd,tkd->kgst', grouped, key_float) / math.sqrt(HD)
    positions = jnp.arange(SEQ)
    causal = positions[:, None] >= positions[None, :]
    scores = jnp.where(causal, scores, -1e+30)
    highest = lax.optimization_barrier(jnp.max(scores, axis=-1, keepdims=True))
    weights = jnp.exp(scores - highest)
    probability = (weights / lax.optimization_barrier(jnp.sum(weights, axis=-1, keepdims=True))).astype(jnp.bfloat16)
    mixed_heads = jnp.einsum('kgst,tkd->skgd', probability.astype(jnp.float32), value_float)
    return mixed_heads.astype(jnp.bfloat16).reshape(SEQ, HEADS * HD)

def reference(residual, query_states, key_states, value_states, prompt_perm, ablated_heads, out_weight, rms_gain, gate_weight, up_weight, down_weight):
    head_rows = lax.map(attend_prompt, (query_states, key_states, value_states))
    stacked = head_rows.reshape(PROMPTS, SEQ, HEADS, HD)
    swapped = jnp.take(stacked, prompt_perm, axis=0)
    chosen = jnp.any(jnp.arange(HEADS)[:, None] == ablated_heads[None, :], axis=1)
    ablated = jnp.where(chosen[None, None, :, None], swapped, stacked).reshape(PROMPTS * SEQ, HEADS * HD)
    attn_float = jnp.dot(ablated, out_weight, preferred_element_type=jnp.float32)
    attn_out = attn_float.astype(jnp.bfloat16)
    hidden_state = residual.reshape(PROMPTS * SEQ, D).astype(jnp.float32) + attn_float
    inverse = lax.rsqrt(lax.optimization_barrier(jnp.mean(hidden_state * hidden_state, axis=1)) + 1e-05)
    normed = (hidden_state * inverse[:, None] * rms_gain.astype(jnp.float32)[None, :]).astype(jnp.bfloat16)
    gate_part = jnp.dot(normed, gate_weight, preferred_element_type=jnp.float32)
    up_part = jnp.dot(normed, up_weight, preferred_element_type=jnp.float32)
    hidden = (jax.nn.silu(gate_part) * up_part).astype(jnp.bfloat16)
    slice_width = FF // N_BATCH
    slices = hidden.reshape(PROMPTS * SEQ, N_BATCH, slice_width).transpose(1, 0, 2)
    blocks = down_weight.reshape(N_BATCH, slice_width, D)

    def add_part(running, operands):
        part_value = jnp.dot(operands[0], operands[1], preferred_element_type=jnp.float32).astype(jnp.bfloat16)
        return (running + part_value.astype(jnp.float32), None)
    running, unused = lax.scan(add_part, jnp.zeros((PROMPTS * SEQ, D), jnp.float32), (slices, blocks))
    return (attn_out.reshape(PROMPTS, SEQ, D), running.astype(jnp.bfloat16).reshape(PROMPTS, SEQ, D))
```

```python
import functools
import math

import jax
import jax.numpy as jnp
from jax import lax
from jax.experimental import pallas as pl
from jax.experimental.pallas import tpu as pltpu
from jax.sharding import PartitionSpec as P

D = 8192
HEADS = 32
KV = 4
HD = 128
R = 16
LAG = 2
BF16, F32 = jnp.bfloat16, jnp.float32


def remote(src, dst, sems, at, **peer):
    return pltpu.make_async_remote_copy(
        src_ref=src,
        dst_ref=dst,
        send_sem=sems[0].at[at],
        recv_sem=sems[1].at[at],
        device_id=peer,
        device_id_type=pl.DeviceIdType.MESH,
    )


def layer_kernel(
    nb, n, slots,
    perm_ref, ablated_ref, res_hbm, q_hbm, k_hbm, v_hbm, wo_hbm, gain_ref, wg_hbm, wu_hbm, wd_hbm,
    attn_ref, mlp_ref,
    res_buf, q_buf, k_buf, v_buf, wo_buf, wg_buf, wu_buf, wd_buf,
    pmat, line, rows,
    part_a, near_a, mid_a, far_a, part_m, near_m, mid_m, far_m,
    x_all, own_sq, got_sq, inv, own, got, hid,
    small_sem, big_sem, gate_sem, up_sem,
    line_s, line_r, owner_s, owner_r,
    na_s, na_r, fa_s, fa_r, nm_s, nm_r, fm_s, fm_r,
    agf_s, agf_r, agn_s, agn_r, sq_s, sq_r, inv_s, inv_r, sum_s, sum_r, hid_s, hid_r,
):
    b, m = lax.axis_index("batch"), lax.axis_index("mp")
    chips = nb // 2
    core, chip = lax.rem(b, 2), lax.div(b, 2)
    mate = b + 1 - 2 * core
    length, cols_d = res_buf.shape
    chunks = length // R
    _, _, owners, _, owned = line.shape
    pieces, _, w = wg_buf.shape
    half = chips * R
    all_rows = nb * R
    heads_here = q_buf.shape[1] // HD
    ends = (n - 1, 0)
    end = (n - 1) * (1 - core)

    kv = lax.div(m * heads_here, HEADS // KV)
    kv = pl.ds(pl.multiple_of(kv * HD, HD), HD)
    small = [
        pltpu.make_async_copy(src, dst, small_sem.at[i])
        for i, (src, dst) in enumerate(
            (
                (q_hbm.at[0], q_buf),
                (k_hbm.at[0, :, kv], k_buf),
                (v_hbm.at[0, :, kv], v_buf),
                (res_hbm.at[0], res_buf),
            )
        )
    ]
    load_wo = pltpu.make_async_copy(wo_hbm, wo_buf, big_sem.at[0])
    load_wd = pltpu.make_async_copy(wd_hbm, wd_buf, big_sem.at[1])

    def piece(c):
        return pl.ds(0, w) if pieces == 1 else pl.ds(pl.multiple_of(c * w, w), w)

    def load_up(c):
        return (
            pltpu.make_async_copy(wg_hbm.at[:, piece(c)], wg_buf.at[c], gate_sem.at[c]),
            pltpu.make_async_copy(wu_hbm.at[:, piece(c)], wu_buf.at[c], up_sem.at[c]),
        )

    for copy in small:
        copy.start()
    barrier = pltpu.get_barrier_semaphore()
    for axis, at, size in (("mp", m, n), ("batch", b, nb)):
        for k in range(1, size):
            pl.semaphore_signal(
                barrier,
                inc=1,
                device_id={axis: lax.rem(at + k, size)},
                device_id_type=pl.DeviceIdType.MESH,
            )
    load_wo.start()
    for c in range(pieces):
        for copy in load_up(c):
            copy.start()
    load_wd.start()

    at_row = lax.broadcasted_iota(jnp.int32, (R, all_rows), 0)
    at_col = lax.broadcasted_iota(jnp.int32, (R, all_rows), 1)
    for slot in range(nb):
        source = perm_ref[2 * (slot % chips) + slot // chips]
        source = lax.rem(source, 2) * chips + lax.div(source, 2)
        hit = at_col - at_row == source * R
        pmat[slot * R : (slot + 1) * R, :] = jnp.where(hit, 1.0, 0.0).astype(BF16)

    for copy in small[:3]:
        copy.wait()
    q = jnp.concatenate([q_buf[:, h * HD : (h + 1) * HD] for h in range(heads_here)], axis=0)
    scores = lax.dot_general(
        q, k_buf[...], (((1,), (1,)), ((), ())), preferred_element_type=F32
    ) / math.sqrt(HD)
    position = lax.rem(lax.broadcasted_iota(jnp.int32, scores.shape, 0), length)
    causal = position >= lax.broadcasted_iota(jnp.int32, scores.shape, 1)
    scores = jnp.where(causal, scores, -1e30)
    weights = jnp.exp(scores - jnp.max(scores, axis=-1, keepdims=True))
    probability = weights / jnp.sum(weights, axis=-1, keepdims=True)
    mixed = jnp.dot(probability.astype(BF16), v_buf[...], preferred_element_type=F32).astype(BF16)
    for k in range(chunks):
        for h in range(heads_here):
            at = h * HD % owned
            line[m, k, h * HD // owned, :, at : at + HD] = mixed[
                h * length + k * R : h * length + (k + 1) * R
            ]

    def line_copy(source, j, k, peer):
        block = line.at[source, k]
        return remote(block, block, (line_s, line_r), (k, j - 1), mp=peer)

    def owner_copy(source, j, i, k, sender, peer):
        return pltpu.make_async_remote_copy(
            src_ref=line.at[source, k, i],
            dst_ref=rows.at[k, lax.rem(sender, 2), lax.div(sender, 2)],
            send_sem=owner_s.at[k, j, i],
            recv_sem=owner_r.at[k, sender],
            device_id={"batch": peer},
            device_id_type=pl.DeviceIdType.MESH,
        )

    pl.semaphore_wait(barrier, n + nb - 2)
    for k in range(chunks):
        for j in range(1, n):
            line_copy(m, j, k, lax.rem(m + j, n)).start()

    def spread_heads(k):
        for j in range(n):
            source = lax.rem(m + n - j, n)
            if j > 0:
                line_copy(source, j, k, source).wait_recv()
            for i in range(owners):
                owner = source * owners + i

                @pl.when(owner != b)
                def _(source=source, j=j, i=i, owner=owner):
                    owner_copy(source, j, i, k, b, owner).start()

                @pl.when(owner == b)
                def _(source=source, i=i):
                    rows[k, core, chip] = line[source, k, i]

    def near_copy(k, part, near, sems):
        return remote(part.at[k, 1 - core], near.at[k], sems, k, batch=mate)

    def far_copy(k, j, mid, far, sems, peer):
        return remote(mid.at[k, j - 1], far.at[k, j - 1], sems, (k, j - 1), batch=peer)

    scatter_a = (part_a, near_a, mid_a, far_a, (na_s, na_r), (fa_s, fa_r))
    scatter_m = (part_m, near_m, mid_m, far_m, (nm_s, nm_r), (fm_s, fm_r))

    def scatter_far(k, bufs):
        part, near, mid, far, near_sems, far_sems = bufs
        near_copy(k, part, near, near_sems).wait_recv()
        for j in range(1, chips):
            target = lax.rem(chip + j, chips)
            mid[k, j - 1] = (part[k, core, target].astype(F32) + near[k, target].astype(F32)).astype(
                BF16
            )
            far_copy(k, j, mid, far, far_sems, 2 * target + core).start()

    def scatter_total(k, bufs):
        part, near, mid, far, near_sems, far_sems = bufs
        total = part[k, core, chip].astype(F32) + near[k, chip].astype(F32)
        for j in range(1, chips):
            far_copy(k, j, mid, far, far_sems, mate).wait_recv()
            total = total + far[k, j - 1].astype(F32)
        return total

    def multiply_into(k, part, x, weight):
        tile = 512 if cols_d % 512 == 0 else cols_d

        def one(i, carry):
            at = pl.ds(pl.multiple_of(i * tile, tile), tile)
            made = jnp.dot(x, weight[:, at], preferred_element_type=F32).astype(BF16)
            part[k, :, :, :, at] = made.reshape(2, chips, R, tile)
            return carry

        lax.fori_loop(0, cols_d // tile, one, 0)

    def project(k):
        for j in range(1, nb):
            other = lax.rem(b + j, nb)
            owner_copy(m, 0, 0, k, other, other).wait_recv()

        @pl.when(k == 0)
        def _():
            load_wo.wait()

        x = rows[k].reshape(all_rows, owned)
        other = jnp.dot(pmat[...], x, preferred_element_type=F32)
        head = lax.broadcasted_iota(jnp.int32, (all_rows, owned), 1) // HD + b * (owned // HD)
        chosen = head == ablated_ref[0]
        for i in range(1, ablated_ref.shape[0]):
            chosen = chosen | (head == ablated_ref[i])
        x = jnp.where(chosen, other, x.astype(F32)).astype(BF16)
        multiply_into(k, part_a, x, wo_buf)
        near_copy(k, part_a, near_a, (na_s, na_r)).start()

    def rows_at(k):
        return pl.ds(pl.multiple_of(k * R, R), R)

    def gather_far(k, j, source, peer):
        block = x_all.at[k, core, source]
        return remote(block, block, (agf_s, agf_r), (k, j - 1), batch=peer)

    def gather_near(k, j, which, source):
        block = x_all.at[k, which, source]
        return remote(block, block, (agn_s, agn_r), (k, j), batch=mate)

    def square_copy(k, source, peer):
        return pltpu.make_async_remote_copy(
            src_ref=own_sq.at[k],
            dst_ref=got_sq.at[k, source],
            send_sem=sq_s.at[k],
            recv_sem=sq_r.at[k, source],
            device_id={"mp": peer},
            device_id_type=pl.DeviceIdType.MESH,
        )

    def inverse_copy(k, j, source, peer):
        block = inv.at[k, source]
        return pltpu.make_async_remote_copy(
            src_ref=block,
            dst_ref=block,
            send_sem=inv_s.at[k, j - 1],
            recv_sem=inv_r.at[k, source],
            device_id={"batch": peer},
            device_id_type=pl.DeviceIdType.MESH,
        )

    def normalize(k):
        total = scatter_total(k, scatter_a)
        attn_ref[0, rows_at(k), :] = total.astype(BF16)
        state = res_buf[rows_at(k), :].astype(F32) + total
        x_all[k, core, chip] = (state * gain_ref[...].reshape(1, cols_d)).astype(BF16)
        for j in range(1, chips):
            gather_far(k, j, chip, 2 * lax.rem(chip + j, chips) + core).start()
        gather_near(k, 0, core, chip).start()
        squares = jnp.sum(state * state, axis=1, keepdims=True)
        own_sq[k] = jnp.broadcast_to(squares, (R, 128))

        @pl.when(m != end)
        def _():
            square_copy(k, m, end).start()

    def gather_rest(k):
        for j in range(1, chips):
            source = lax.rem(chip + chips - j, chips)
            gather_far(k, j, source, mate).wait_recv()
            gather_near(k, j, core, source).start()

        @pl.when(m == end)
        def _():
            total = own_sq[k]
            for j in range(1, n):
                source = lax.rem(m + j, n)
                square_copy(k, source, source).wait_recv()
                total = total + got_sq[k, source]
            inv[k, chip] = lax.rsqrt(total / D + 1e-05)
            for j in range(1, nb):
                inverse_copy(k, j, chip, lax.rem(b + j, nb)).start()

    pos_of = (m, n - 1 - m)
    way_of = (1, -1)

    def sum_copy(d, u, peer):
        return remote(own.at[u, d], got.at[d, u], (sum_s, sum_r), (d, u), mp=peer)

    def hid_copy(d, k, c, peer):
        block = hid.at[k, d, :, piece(c)]
        return remote(block, block, (hid_s, hid_r), (d, k * pieces + c), mp=peer)

    def unit(t):
        k, c = lax.div(t, slots), lax.rem(t, slots)
        return k, c, (t >= 0) & (t < chunks * slots) & (c < pieces)

    def step(i, carry):
        t = i - slots
        k, c, here = unit(t)

        @pl.when(here)
        def _():
            @pl.when(c == 0)
            def _():
                for j in range(chips):
                    source = lax.rem(chip + chips - j, chips)
                    gather_near(k, j, 1 - core, source).wait_recv()

            @pl.when(k == 0)
            def _():
                for copy in load_up(c):
                    copy.wait()

            x = x_all[k].reshape(all_rows, cols_d)
            for i, weight in enumerate((wg_buf, wu_buf)):
                made = jnp.dot(x, weight[c], preferred_element_type=F32).astype(BF16)
                for d in range(2):
                    own[k * pieces + c, d, i] = made[d * half : (d + 1) * half]

        for d in range(2):
            pos, way = pos_of[d], way_of[d]
            k, c, here = unit(t - LAG * pos)
            u = k * pieces + c

            @pl.when(here & (pos == 0))
            def _(d=d, u=u, way=way):
                sum_copy(d, u, m + way).start()

            @pl.when(here & (pos > 0) & (pos < n - 1))
            def _(d=d, u=u, way=way):
                sum_copy(d, u, m - way).wait_recv()
                own[u, d] = (own[u, d].astype(F32) + got[d, u].astype(F32)).astype(BF16)
                sum_copy(d, u, m + way).start()

            @pl.when(here & (pos == n - 1))
            def _(d=d, k=k, c=c, u=u, way=way):
                @pl.when(c == 0)
                def _():
                    for j in range(chips):
                        source = lax.rem(chip + j, chips)

                        @pl.when((core != d) | (j > 0))
                        def _(source=source):
                            inverse_copy(k, 1, source, mate).wait_recv()

                sum_copy(d, u, m - way).wait_recv()
                inverse = inv[k].reshape(half, 128)[:, :1]
                gate = (own[u, d, 0].astype(F32) + got[d, u, 0].astype(F32)) * inverse
                up = (own[u, d, 1].astype(F32) + got[d, u, 1].astype(F32)) * inverse
                hid[k, d, :, piece(c)] = (gate / (1.0 + jnp.exp(-gate)) * up).astype(BF16)
                hid_copy(d, k, c, m - way).start()

            k, c, here = unit(t - LAG * (2 * (n - 1) - pos))

            @pl.when(here & (pos < n - 1))
            def _(d=d, k=k, c=c, way=way, pos=pos):
                hid_copy(d, k, c, m + way).wait_recv()

                @pl.when(pos > 0)
                def _():
                    hid_copy(d, k, c, m - way).start()

        k, s = lax.div(i, slots), lax.rem(i, slots)
        here = k < chunks
        for at, do in (
            (0, project),
            (1, lambda k: scatter_far(k, scatter_a)),
            (2, normalize),
            (3, gather_rest),
        ):

            @pl.when(here & (s == at))
            def _(do=do, k=k):
                do(k)

        @pl.when((k + 1 < chunks) & (s == 4))
        def _():
            spread_heads(k + 1)

        back = t - LAG * 2 * (n - 1) - (pieces - 1)
        k, s = lax.div(back, slots), lax.rem(back, slots)
        here = (back >= 0) & (k < chunks)

        @pl.when(here & (s == 0))
        def _():
            @pl.when(k == 0)
            def _():
                load_wd.wait()

            multiply_into(k, part_m, hid[k].reshape(all_rows, pieces * w), wd_buf)
            near_copy(k, part_m, near_m, (nm_s, nm_r)).start()

        @pl.when(here & (s == 1))
        def _():
            scatter_far(k, scatter_m)

        @pl.when(here & (s == 2))
        def _():
            mlp_ref[0, rows_at(k), :] = scatter_total(k, scatter_m).astype(BF16)

        return carry

    spread_heads(0)
    small[3].wait()
    last = chunks * slots + pieces - 1 + LAG * 2 * (n - 1) + 3
    lax.fori_loop(0, last, step, 0)

    def finish(k, carry):
        for j in range(1, n):
            line_copy(m, j, k, m).wait_send()
        for j in range(n):
            source = lax.rem(m + n - j, n)
            for i in range(owners):

                @pl.when(source * owners + i != b)
                def _(source=source, j=j, i=i):
                    owner_copy(source, j, i, k, b, mate).wait_send()

        for part, near, mid, far, near_sems, far_sems in (scatter_a, scatter_m):
            near_copy(k, part, near, near_sems).wait_send()
            for j in range(1, chips):
                far_copy(k, j, mid, far, far_sems, mate).wait_send()
        for j in range(1, chips):
            gather_far(k, j, chip, mate).wait_send()
        for j in range(chips):
            gather_near(k, j, core, chip).wait_send()

        @pl.when(m != end)
        def _():
            square_copy(k, m, end).wait_send()

        @pl.when(m == end)
        def _():
            for j in range(1, nb):
                inverse_copy(k, j, chip, mate).wait_send()

        def finish_unit(c, carry):
            for d in range(2):
                pos, way = pos_of[d], way_of[d]

                @pl.when(pos < n - 1)
                def _(d=d, way=way):
                    sum_copy(d, k * pieces + c, m + way).wait_send()

                @pl.when(pos > 0)
                def _(d=d, way=way):
                    hid_copy(d, k, c, m - way).wait_send()

            return carry

        return lax.fori_loop(0, pieces, finish_unit, carry)

    lax.fori_loop(0, chunks, finish, 0)


def body(
    residual, query_states, key_states, value_states, prompt_perm, ablated_heads, out_weight,
    rms_gain, gate_weight, up_weight, down_weight,
):
    _, length, cols_d = residual.shape
    nb, n = lax.axis_size("batch"), lax.axis_size("mp")
    chips = nb // 2
    chunks = length // R
    owned = out_weight.shape[0]
    columns = query_states.shape[2]
    owners = columns // owned
    width = gate_weight.shape[1]
    w = 256 if width % 256 == 0 else width
    pieces = width // w
    slots = max(pieces, 6)
    units = chunks * pieces
    half = chips * R
    vmem = pl.BlockSpec(memory_space=pltpu.VMEM)
    smem = pl.BlockSpec(memory_space=pltpu.SMEM)
    anywhere = pl.BlockSpec(memory_space=pl.ANY)
    dma = pltpu.SemaphoreType.DMA

    def scatter_bufs():
        return [
            pltpu.VMEM((chunks, 2, chips, R, cols_d), BF16),
            pltpu.VMEM((chunks, chips, R, cols_d), BF16),
            pltpu.VMEM((chunks, chips - 1, R, cols_d), BF16),
            pltpu.VMEM((chunks, chips - 1, R, cols_d), BF16),
        ]

    out = jax.ShapeDtypeStruct((1, length, cols_d), BF16)
    return pl.pallas_call(
        functools.partial(layer_kernel, nb, n, slots),
        in_specs=[smem, smem] + [anywhere] * 5 + [vmem] + [anywhere] * 3,
        out_specs=[vmem, vmem],
        out_shape=[out, out],
        scratch_shapes=[
            pltpu.VMEM((length, cols_d), BF16),
            pltpu.VMEM((length, columns), BF16),
            pltpu.VMEM((length, HD), BF16),
            pltpu.VMEM((length, HD), BF16),
            pltpu.VMEM((owned, cols_d), BF16),
            pltpu.VMEM((pieces, cols_d, w), BF16),
            pltpu.VMEM((pieces, cols_d, w), BF16),
            pltpu.VMEM((width, cols_d), BF16),
            pltpu.VMEM((nb * R, nb * R), BF16),
            pltpu.VMEM((n, chunks, owners, R, owned), BF16),
            pltpu.VMEM((chunks, 2, chips, R, owned), BF16),
            *scatter_bufs(),
            *scatter_bufs(),
            pltpu.VMEM((chunks, 2, chips, R, cols_d), BF16),
            pltpu.VMEM((chunks, R, 128), F32),
            pltpu.VMEM((chunks, n, R, 128), F32),
            pltpu.VMEM((chunks, chips, R, 128), F32),
            pltpu.VMEM((units, 2, 2, half, w), BF16),
            pltpu.VMEM((2, units, 2, half, w), BF16),
            pltpu.VMEM((chunks, 2, half, width), BF16),
            dma((4,)),
            dma((2,)),
            dma((pieces,)),
            dma((pieces,)),
            *[dma((chunks, n - 1))] * 2,
            dma((chunks, n, owners)),
            dma((chunks, nb)),
            *[dma((chunks,)), dma((chunks,)), dma((chunks, chips - 1)), dma((chunks, chips - 1))] * 2,
            *[dma((chunks, chips - 1))] * 2,
            *[dma((chunks, chips))] * 2,
            dma((chunks,)),
            dma((chunks, n)),
            dma((chunks, nb - 1)),
            dma((chunks, chips)),
            *[dma((2, units))] * 4,
        ],
        compiler_params=pltpu.CompilerParams(
            collective_id=1, has_side_effects=True, vmem_limit_bytes=60 * 2**20
        ),
    )(
        prompt_perm, ablated_heads, residual, query_states, key_states, value_states, out_weight,
        rms_gain, gate_weight, up_weight, down_weight,
    )


def solution(mesh):
    placed = (
        P("batch", None, "mp"),
        P("batch", None, "mp"),
        P("batch", None, None),
        P("batch", None, None),
        P(),
        P(),
        P("batch", "mp"),
        P("mp"),
        P("mp", "batch"),
        P("mp", "batch"),
        P("batch", "mp"),
    )
    return jax.shard_map(
        body,
        mesh=mesh,
        in_specs=placed,
        out_specs=(P("batch", None, "mp"), P("batch", None, "mp")),
        check_vma=False,
    )
```

```python
import functools
import math

import jax
import jax.numpy as jnp
from jax import lax
from jax.experimental import pallas as pl
from jax.experimental.pallas import tpu as pltpu
from jax.sharding import PartitionSpec as P

D = 8192
HEADS = 32
KV = 4
HD = 128
R = 16
LAG = 3
LEAD = 20
VMEM = 60 * 2**20
BF16, F32 = jnp.bfloat16, jnp.float32


def remote(src, dst, send_sem, recv_sem, **peer):
    return pltpu.make_async_remote_copy(
        src_ref=src,
        dst_ref=dst,
        send_sem=send_sem,
        recv_sem=recv_sem,
        device_id=peer,
        device_id_type=pl.DeviceIdType.MESH,
    )


def layer_kernel(
    nb, n, slots, w, joined,
    perm_ref, ablated_ref, res_hbm, q_hbm, k_hbm, v_hbm, wo_hbm, gain_ref, wg_hbm, wu_hbm, wd_hbm,
    attn_ref, mlp_ref,
    res_buf, q_buf, k_buf, v_buf, wo_buf, w_buf, wd_buf,
    pmat, line, rows,
    part_a, near_a, mid_a, far_a, part_m, near_m, mid_m, far_m,
    x_all, own_sq, got_sq, inv, own, got, hid,
    small_sem, big_sem,
    line_s, line_r, owner_s, owner_r,
    na_s, na_r, fa_s, fa_r, nm_s, nm_r, fm_s, fm_r,
    agf_s, agf_r, agn_s, agn_r, sq_s, sq_r, inv_s, inv_r, sum_s, sum_r, hid_s, hid_r,
):
    b, m = lax.axis_index("batch"), lax.axis_index("mp")
    chips = nb // 2
    core, chip = lax.rem(b, 2), lax.div(b, 2)
    mate = b + 1 - 2 * core
    my_slot = core * chips + chip
    length, cols_d = res_buf.shape
    chunks = length // R
    _, _, owners, _, owned = line.shape
    pieces = w_buf.shape[0]
    reuse = sum_r.shape[1]
    half = chips * R
    all_rows = nb * R
    heads_here = q_buf.shape[1] // HD
    end = (n - 1) * (1 - core)

    def slot_of(device):
        return lax.rem(device, 2) * chips + lax.div(device, 2)

    kv = lax.div(m * heads_here, HEADS // KV)
    kv = pl.ds(pl.multiple_of(kv * HD, HD), HD)
    small = [
        pltpu.make_async_copy(src, dst, small_sem.at[i])
        for i, (src, dst) in enumerate(
            (
                (q_hbm.at[0], q_buf),
                (k_hbm.at[0, :, kv], k_buf),
                (v_hbm.at[0, :, kv], v_buf),
                (res_hbm.at[0], res_buf),
            )
        )
    ]
    load_wo = pltpu.make_async_copy(wo_hbm, wo_buf, big_sem.at[0])
    load_wd = pltpu.make_async_copy(wd_hbm, wd_buf, big_sem.at[1])

    def piece(c):
        return pl.ds(0, w) if pieces == 1 else pl.ds(pl.multiple_of(c * w, w), w)

    for copy in small:
        copy.start()
    barrier = pltpu.get_barrier_semaphore()
    for axis, at, size in (("mp", m, n), ("batch", b, nb)):
        for k in range(1, size):
            pl.semaphore_signal(
                barrier,
                inc=1,
                device_id={axis: lax.rem(at + k, size)},
                device_id_type=pl.DeviceIdType.MESH,
            )
    load_wo.start()
    for c in range(pieces):
        for i, src in enumerate((wg_hbm, wu_hbm)):
            dst = w_buf.at[c, :, pl.ds(i * w, w)] if joined else w_buf.at[c, i]
            pltpu.make_async_copy(src.at[:, piece(c)], dst, big_sem.at[2]).start()
    load_wd.start()

    at_row = lax.broadcasted_iota(jnp.int32, (R, all_rows), 0)
    at_col = lax.broadcasted_iota(jnp.int32, (R, all_rows), 1)
    for slot in range(nb):
        source = slot_of(perm_ref[2 * (slot % chips) + slot // chips])
        hit = at_col - at_row == source * R
        pmat[slot * R : (slot + 1) * R, :] = jnp.where(hit, 1.0, 0.0).astype(BF16)

    for copy in small[:3]:
        copy.wait()
    q = jnp.concatenate([q_buf[:, h * HD : (h + 1) * HD] for h in range(heads_here)], axis=0)
    scores = lax.dot_general(
        q, k_buf[...], (((1,), (1,)), ((), ())), preferred_element_type=F32
    ) / math.sqrt(HD)
    position = lax.rem(lax.broadcasted_iota(jnp.int32, scores.shape, 0), length)
    causal = position >= lax.broadcasted_iota(jnp.int32, scores.shape, 1)
    scores = jnp.where(causal, scores, -1e30)
    weights = jnp.exp(scores - jnp.max(scores, axis=-1, keepdims=True))
    probability = weights / jnp.sum(weights, axis=-1, keepdims=True)
    mixed = jnp.dot(probability.astype(BF16), v_buf[...], preferred_element_type=F32).astype(BF16)
    for k in range(chunks):
        for h in range(heads_here):
            at = h * HD % owned
            line[m, k, h * HD // owned, :, at : at + HD] = mixed[
                h * length + k * R : h * length + (k + 1) * R
            ]

    def line_copy(source, j, k, peer):
        block = line.at[source, k]
        return remote(block, block, line_s.at[0], line_r.at[k, j - 1], mp=peer)

    def line_send(k):
        for j in range(1, n):
            line_copy(m, j, k, lax.rem(m + j, n)).start()

    def spread_heads(k):
        for j in range(n):
            source = lax.rem(m + n - j, n)
            if j > 0:
                line_copy(source, j, k, source).wait_recv()
            for i in range(owners):
                owner = source * owners + i

                @pl.when(owner != b)
                def _(source=source, i=i, owner=owner):
                    remote(
                        line.at[source, k, i],
                        rows.at[k, my_slot],
                        owner_s.at[k],
                        owner_r.at[k],
                        batch=owner,
                    ).start()

                @pl.when(owner == b)
                def _(source=source, i=i):
                    rows[k, my_slot] = line[source, k, i]

    def all_owners(k):
        block = rows.at[k, pl.ds(0, nb - 1)]
        return remote(block, block, owner_s.at[k], owner_r.at[k], batch=mate)

    scatter_a = (part_a, near_a, mid_a, far_a, na_s, na_r, fa_s, fa_r)
    scatter_m = (part_m, near_m, mid_m, far_m, nm_s, nm_r, fm_s, fm_r)

    def near_copy(k, bufs):
        part, near, mid, far, near_s, near_r, far_s, far_r = bufs
        block = part.at[k, pl.ds((1 - core) * chips, chips)]
        return remote(block, near.at[k], near_s.at[0], near_r.at[k], batch=mate)

    def scatter_far(k, bufs):
        part, near, mid, far, near_s, near_r, far_s, far_r = bufs
        near_copy(k, bufs).wait_recv()
        for j in range(1, chips):
            target = lax.rem(chip + j, chips)
            mid[k, j - 1] = (
                part[k, core * chips + target].astype(F32) + near[k, target].astype(F32)
            ).astype(BF16)
            remote(
                mid.at[k, j - 1],
                far.at[k, j - 1],
                far_s.at[0],
                far_r.at[k],
                batch=2 * target + core,
            ).start()

    def scatter_total(k, bufs):
        part, near, mid, far, near_s, near_r, far_s, far_r = bufs
        total = part[k, my_slot].astype(F32) + near[k, chip].astype(F32)
        remote(mid.at[k], far.at[k], far_s.at[0], far_r.at[k], batch=mate).wait_recv()
        for j in range(1, chips):
            total = total + far[k, j - 1].astype(F32)
        return total

    def multiply_into(k, bufs, left, weight):
        tile = 512 if cols_d % 512 == 0 else cols_d

        def one(i, carry):
            at = pl.ds(pl.multiple_of(i * tile, tile), tile)
            made = jnp.dot(left(), weight[:, at], preferred_element_type=F32).astype(BF16)
            bufs[0][k, :, :, at] = made.reshape(nb, R, tile)
            return carry

        lax.fori_loop(0, cols_d // tile, one, 0)
        near_copy(k, bufs).start()

    def project(k):
        all_owners(k).wait_recv()

        @pl.when(k == 0)
        def _():
            load_wo.wait()

        x = rows[k].reshape(all_rows, owned)
        other = jnp.dot(pmat[...], x, preferred_element_type=F32)
        head = lax.broadcasted_iota(jnp.int32, (all_rows, owned), 1) // HD + b * (owned // HD)
        chosen = head == ablated_ref[0]
        for i in range(1, ablated_ref.shape[0]):
            chosen = chosen | (head == ablated_ref[i])
        x = jnp.where(chosen, other, x.astype(F32)).astype(BF16)
        multiply_into(k, scatter_a, lambda: x, wo_buf)

    def rows_at(k):
        return pl.ds(pl.multiple_of(k * R, R), R)

    def gather_far(k, j, source, peer):
        block = x_all.at[k, core * chips + source]
        return remote(block, block, agf_s.at[0], agf_r.at[k, j - 1], batch=peer)

    def gather_near(k, block):
        return remote(block, block, agn_s.at[0], agn_r.at[k], batch=mate)

    def gather_near_all(k):
        return gather_near(k, x_all.at[k, pl.ds((1 - core) * chips, chips)])

    def square_copy(k):
        place = lax.rem(m + n - end, n) - 1
        return remote(own_sq.at[k], got_sq.at[k, place], sq_s.at[0], sq_r.at[k], mp=end)

    def inverse_wait(k, count):
        block = inv.at[pl.ds(0, count)]
        return remote(block, block, inv_s.at[k], inv_r.at[k], batch=mate)

    def normalize(k):
        total = scatter_total(k, scatter_a)
        attn_ref[0, rows_at(k), :] = total.astype(BF16)
        state = res_buf[rows_at(k), :].astype(F32) + total
        x_all[k, my_slot] = (state * gain_ref[...].reshape(1, cols_d)).astype(BF16)
        for j in range(1, chips):
            gather_far(k, j, chip, 2 * lax.rem(chip + j, chips) + core).start()
        gather_near(k, x_all.at[k, my_slot]).start()
        squares = jnp.sum(state * state, axis=1, keepdims=True)
        own_sq[k] = jnp.broadcast_to(squares, (R, 128))

        @pl.when(m != end)
        def _():
            square_copy(k).start()

    def gather_rest(k):
        for j in range(1, chips):
            source = lax.rem(chip + chips - j, chips)
            gather_far(k, j, source, mate).wait_recv()
            gather_near(k, x_all.at[k, core * chips + source]).start()

        @pl.when(m == end)
        def _():
            total = own_sq[k]
            remote(got_sq.at[k], got_sq.at[k], sq_s.at[0], sq_r.at[k], mp=end).wait_recv()
            for j in range(1, n):
                total = total + got_sq[k, j - 1]
            mine = k * chips + chip
            inv[mine] = lax.rsqrt(total / D + 1e-05)
            for j in range(1, nb):
                remote(
                    inv.at[mine],
                    inv.at[mine],
                    inv_s.at[k],
                    inv_r.at[k],
                    batch=lax.rem(b + j, nb),
                ).start()

    pos_of = (m, n - 1 - m)
    way_of = (1, -1)

    def sum_copy(d, u, peer):
        at = lax.rem(u, reuse)
        return remote(own.at[d, u], got.at[d, u], sum_s.at[d], sum_r.at[d, at], mp=peer)

    def hid_copy(d, k, c, peer):
        block = hid.at[d, k, :, piece(c)]
        at = lax.rem(k * pieces + c, reuse)
        return remote(block, block, hid_s.at[d], hid_r.at[d, at], mp=peer)

    def unit(v):
        k, c = lax.div(v, slots), lax.rem(v, slots)
        return k, c, (v >= 0) & (v < chunks * slots) & (c < pieces)

    def step(i, carry):
        t = i - LEAD
        k, c, here = unit(t)

        @pl.when(here)
        def _():
            @pl.when(c == 0)
            def _():
                gather_near_all(k).wait_recv()

                @pl.when(k == 0)
                def _():
                    pltpu.make_async_copy(w_buf, w_buf, big_sem.at[2]).wait()

            x = x_all[k].reshape(all_rows, cols_d)
            u = k * pieces + c
            if joined:
                made = jnp.dot(x, w_buf[c], preferred_element_type=F32).astype(BF16)
                for d in range(2):
                    own[d, u] = made[d * half : (d + 1) * half]
            else:
                for which in range(2):
                    made = jnp.dot(x, w_buf[c, which], preferred_element_type=F32).astype(BF16)
                    for d in range(2):
                        own[d, u, which] = made[d * half : (d + 1) * half]

        for d in range(2):
            pos, way = pos_of[d], way_of[d]
            k, c, here = unit(t - LAG * pos)
            u = k * pieces + c

            @pl.when(here & (pos == 0))
            def _(d=d, u=u, way=way):
                sum_copy(d, u, m + way).start()

            @pl.when(here & (pos > 0) & (pos < n - 1))
            def _(d=d, u=u, way=way):
                sum_copy(d, u, m - way).wait_recv()
                own[d, u] = (own[d, u].astype(F32) + got[d, u].astype(F32)).astype(BF16)
                sum_copy(d, u, m + way).start()

            @pl.when(here & (pos == n - 1))
            def _(d=d, k=k, c=c, u=u, way=way):
                @pl.when(c == 0)
                def _():
                    @pl.when(core == d)
                    def _():
                        inverse_wait(k, chips - 1).wait_recv()

                    @pl.when(core != d)
                    def _():
                        inverse_wait(k, chips).wait_recv()

                sum_copy(d, u, m - way).wait_recv()
                inverse = inv[pl.ds(k * chips, chips)].reshape(half, 128)[:, :1]
                summed = own[d, u].astype(F32) + got[d, u].astype(F32)
                gate = (summed[:, :w] if joined else summed[0]) * inverse
                up = (summed[:, w:] if joined else summed[1]) * inverse
                hid[d, k, :, piece(c)] = (gate / (1.0 + jnp.exp(-gate)) * up).astype(BF16)
                hid_copy(d, k, c, m - way).start()

            k, c, here = unit(t - LAG * (2 * (n - 1) - pos))

            @pl.when(here & (pos < n - 1))
            def _(d=d, k=k, c=c, way=way, pos=pos):
                hid_copy(d, k, c, m + way).wait_recv()

                @pl.when(pos > 0)
                def _():
                    hid_copy(d, k, c, m - way).start()

        def stage(offset, first, do):
            v = t - offset
            k = lax.div(v, slots)

            @pl.when((v >= first * slots) & (k < chunks) & (lax.rem(v, slots) == 0))
            def _():
                do(k)

        done = pieces - 1 + LAG * 2 * (n - 1)

        def start_scatter(k):
            scatter_far(k, scatter_a)

            @pl.when(k == 0)
            def _():
                for later in range(2, chunks):
                    line_send(later)

        def down(k):
            @pl.when(k == 0)
            def _():
                load_wd.wait()

            multiply_into(
                k, scatter_m, lambda: hid[:, k].reshape(all_rows, pieces * w), wd_buf
            )

        def finish_rows(k):
            mlp_ref[0, rows_at(k), :] = scatter_total(k, scatter_m).astype(BF16)

        stage(done, 0, down)
        stage(done + 2, 0, lambda k: scatter_far(k, scatter_m))
        stage(done + 12, 0, finish_rows)
        stage(-LEAD, 0, project)
        stage(-16, 0, start_scatter)
        stage(-26, 1, spread_heads)
        stage(-8, 0, normalize)
        stage(-3, 0, gather_rest)
        return carry

    pl.semaphore_wait(barrier, n + nb - 2)
    line_send(0)
    spread_heads(0)
    if chunks > 1:
        line_send(1)
    small[3].wait()
    last = LEAD + (chunks - 1) * slots + pieces - 1 + LAG * 2 * (n - 1) + 12 + 1
    lax.fori_loop(0, last, step, 0)

    block = line.at[pl.ds(0, n - 1)]
    remote(block, block, line_s.at[0], line_r.at[0, 0], mp=end).wait_send()
    for k in range(chunks):
        all_owners(k).wait_send()
    for part, near, mid, far, near_s, near_r, far_s, far_r in (scatter_a, scatter_m):
        remote(near, near, near_s.at[0], near_r.at[0], batch=mate).wait_send()
        remote(mid, mid, far_s.at[0], far_r.at[0], batch=mate).wait_send()
    remote(mid_a, mid_a, agf_s.at[0], agf_r.at[0, 0], batch=mate).wait_send()
    remote(near_a, near_a, agn_s.at[0], agn_r.at[0], batch=mate).wait_send()

    @pl.when(m != end)
    def _():
        remote(own_sq, own_sq, sq_s.at[0], sq_r.at[0], mp=end).wait_send()

    @pl.when(m == end)
    def _():
        for k in range(chunks):
            inverse_wait(k, nb - 1).wait_send()

    for d in range(2):
        pos, way = pos_of[d], way_of[d]

        @pl.when(pos < n - 1)
        def _(d=d, way=way):
            remote(own.at[d], got.at[d], sum_s.at[d], sum_r.at[d, 0], mp=m + way).wait_send()

        @pl.when(pos > 0)
        def _(d=d, way=way):
            remote(hid.at[d], hid.at[d], hid_s.at[d], hid_r.at[d, 0], mp=m - way).wait_send()


def body(
    residual, query_states, key_states, value_states, prompt_perm, ablated_heads, out_weight,
    rms_gain, gate_weight, up_weight, down_weight,
):
    _, length, cols_d = residual.shape
    nb, n = lax.axis_size("batch"), lax.axis_size("mp")
    chips = nb // 2
    chunks = length // R
    owned = out_weight.shape[0]
    columns = query_states.shape[2]
    owners = columns // owned
    width = gate_weight.shape[1]
    joined = width % 128 == 0
    w = 128 if joined else width
    pieces = width // w
    slots = max(pieces, 14)
    units = chunks * pieces
    reuse = min(units, 2 * LAG * (n - 1) + 1)
    half = chips * R
    pair = (half, 2 * w) if joined else (2, half, w)
    vmem = pl.BlockSpec(memory_space=pltpu.VMEM)
    smem = pl.BlockSpec(memory_space=pltpu.SMEM)
    anywhere = pl.BlockSpec(memory_space=pl.ANY)
    dma = pltpu.SemaphoreType.DMA

    def scatter_bufs():
        return [
            pltpu.VMEM((chunks, nb, R, cols_d), BF16),
            pltpu.VMEM((chunks, chips, R, cols_d), BF16),
            pltpu.VMEM((chunks, chips - 1, R, cols_d), BF16),
            pltpu.VMEM((chunks, chips - 1, R, cols_d), BF16),
        ]

    out = jax.ShapeDtypeStruct((1, length, cols_d), BF16)
    return pl.pallas_call(
        functools.partial(layer_kernel, nb, n, slots, w, joined),
        in_specs=[smem, smem] + [anywhere] * 5 + [vmem] + [anywhere] * 3,
        out_specs=[vmem, vmem],
        out_shape=[out, out],
        scratch_shapes=[
            pltpu.VMEM((length, cols_d), BF16),
            pltpu.VMEM((length, columns), BF16),
            pltpu.VMEM((length, HD), BF16),
            pltpu.VMEM((length, HD), BF16),
            pltpu.VMEM((owned, cols_d), BF16),
            pltpu.VMEM((pieces, cols_d, 2 * w) if joined else (pieces, 2, cols_d, w), BF16),
            pltpu.VMEM((width, cols_d), BF16),
            pltpu.VMEM((nb * R, nb * R), BF16),
            pltpu.VMEM((n, chunks, owners, R, owned), BF16),
            pltpu.VMEM((chunks, nb, R, owned), BF16),
            *scatter_bufs(),
            *scatter_bufs(),
            pltpu.VMEM((chunks, nb, R, cols_d), BF16),
            pltpu.VMEM((chunks, R, 128), F32),
            pltpu.VMEM((chunks, n - 1, R, 128), F32),
            pltpu.VMEM((chunks * chips, R, 128), F32),
            pltpu.VMEM((2, units, *pair), BF16),
            pltpu.VMEM((2, units, *pair), BF16),
            pltpu.VMEM((2, chunks, half, width), BF16),
            dma((4,)),
            dma((3,)),
            dma((1,)),
            dma((chunks, n - 1)),
            dma((chunks,)),
            dma((chunks,)),
            *[dma((1,)), dma((chunks,)), dma((1,)), dma((chunks,))] * 2,
            dma((1,)),
            dma((chunks, chips - 1)),
            dma((1,)),
            dma((chunks,)),
            dma((1,)),
            dma((chunks,)),
            dma((chunks,)),
            dma((chunks,)),
            dma((2,)),
            dma((2, reuse)),
            dma((2,)),
            dma((2, reuse)),
        ],
        compiler_params=pltpu.CompilerParams(
            collective_id=1, has_side_effects=True, vmem_limit_bytes=VMEM
        ),
    )(
        prompt_perm, ablated_heads, residual, query_states, key_states, value_states, out_weight,
        rms_gain, gate_weight, up_weight, down_weight,
    )


def solution(mesh):
    placed = (
        P("batch", None, "mp"),
        P("batch", None, "mp"),
        P("batch", None, None),
        P("batch", None, None),
        P(),
        P(),
        P("batch", "mp"),
        P("mp"),
        P("mp", "batch"),
        P("mp", "batch"),
        P("batch", "mp"),
    )
    return jax.shard_map(
        body,
        mesh=mesh,
        in_specs=placed,
        out_specs=(P("batch", None, "mp"), P("batch", None, "mp")),
        check_vma=False,
    )
```

```python
import functools
import math

import jax
import jax.numpy as jnp
from jax import lax
from jax.experimental import pallas as pl
from jax.experimental.pallas import tpu as pltpu
from jax.sharding import PartitionSpec as P

D = 8192
HEADS = 32
KV = 4
HD = 128
R = 16
LAG = 4
HLAG = 4
LEAD = 20
FINISH = 12
VMEM = 60 * 2**20
BF16, F32 = jnp.bfloat16, jnp.float32


def remote(src, dst, send_sem, recv_sem, **peer):
    return pltpu.make_async_remote_copy(
        src_ref=src,
        dst_ref=dst,
        send_sem=send_sem,
        recv_sem=recv_sem,
        device_id=peer,
        device_id_type=pl.DeviceIdType.MESH,
    )


def layer_kernel(
    nb, n, slots, w, joined,
    perm_ref, ablated_ref, res_hbm, q_hbm, k_hbm, v_hbm, wo_hbm, gain_ref, wg_hbm, wu_hbm, wd_hbm,
    attn_hbm, mlp_hbm,
    attn_buf, mlp_buf, res_buf, q_buf, k_buf, v_buf, wo_buf, w_buf, wd_buf,
    pmat, line, rows, swapped,
    part_a, near_a, mid_a, far_a, part_m, near_m, mid_m, far_m,
    x_all, own_sq, got_sq, inv, own, got, hid,
    small_sem, big_sem, out_sem,
    line_s, line_r, owner_s, owner_r,
    na_s, na_r, fa_s, fa_r, nm_s, nm_r, fm_s, fm_r,
    agf_s, agf_r, agn_s, agn_r, sq_s, sq_r, inv_s, inv_r, sum_s, sum_r, hid_s, hid_r,
):
    b, m = lax.axis_index("batch"), lax.axis_index("mp")
    chips = nb // 2
    core, chip = lax.rem(b, 2), lax.div(b, 2)
    mate = b + 1 - 2 * core
    my_slot = core * chips + chip
    length, cols_d = res_buf.shape
    chunks = length // R
    _, _, owners, _, owned = line.shape
    pieces = w_buf.shape[0]
    reuse = sum_r.shape[1]
    half = chips * R
    all_rows = nb * R
    heads_here = q_buf.shape[1] // HD
    end = (n - 1) * (1 - core)

    def slot_of(device):
        return lax.rem(device, 2) * chips + lax.div(device, 2)

    kv = lax.div(m * heads_here, HEADS // KV)
    kv = pl.ds(pl.multiple_of(kv * HD, HD), HD)
    small = [
        pltpu.make_async_copy(src, dst, small_sem.at[i])
        for i, (src, dst) in enumerate(
            (
                (q_hbm.at[0], q_buf),
                (k_hbm.at[0, :, kv], k_buf),
                (v_hbm.at[0, :, kv], v_buf),
                (res_hbm.at[0], res_buf),
            )
        )
    ]
    load_wo = pltpu.make_async_copy(wo_hbm, wo_buf, big_sem.at[0])
    load_wd = pltpu.make_async_copy(wd_hbm, wd_buf, big_sem.at[1])

    def piece(c):
        return pl.ds(0, w) if pieces == 1 else pl.ds(pl.multiple_of(c * w, w), w)

    for copy in small:
        copy.start()
    barrier = pltpu.get_barrier_semaphore()
    for axis, at, size in (("mp", m, n), ("batch", b, nb)):
        for k in range(1, size):
            pl.semaphore_signal(
                barrier,
                inc=1,
                device_id={axis: lax.rem(at + k, size)},
                device_id_type=pl.DeviceIdType.MESH,
            )
    load_wo.start()
    for c in range(pieces):
        for i, src in enumerate((wg_hbm, wu_hbm)):
            dst = w_buf.at[c, :, pl.ds(i * w, w)] if joined else w_buf.at[c, i]
            pltpu.make_async_copy(src.at[:, piece(c)], dst, big_sem.at[2]).start()
    load_wd.start()

    at_row = lax.broadcasted_iota(jnp.int32, (R, all_rows), 0)
    at_col = lax.broadcasted_iota(jnp.int32, (R, all_rows), 1)
    for slot in range(nb):
        source = slot_of(perm_ref[2 * (slot % chips) + slot // chips])
        hit = at_col - at_row == source * R
        pmat[slot * R : (slot + 1) * R, :] = jnp.where(hit, 1.0, 0.0).astype(BF16)

    for copy in small[:3]:
        copy.wait()
    q = jnp.concatenate([q_buf[:, h * HD : (h + 1) * HD] for h in range(heads_here)], axis=0)
    scores = lax.dot_general(
        q, k_buf[...], (((1,), (1,)), ((), ())), preferred_element_type=F32
    ) / math.sqrt(HD)
    position = lax.rem(lax.broadcasted_iota(jnp.int32, scores.shape, 0), length)
    causal = position >= lax.broadcasted_iota(jnp.int32, scores.shape, 1)
    scores = jnp.where(causal, scores, -1e30)
    weights = jnp.exp(scores - jnp.max(scores, axis=-1, keepdims=True))
    probability = weights / jnp.sum(weights, axis=-1, keepdims=True)
    mixed = jnp.dot(probability.astype(BF16), v_buf[...], preferred_element_type=F32).astype(BF16)
    for k in range(chunks):
        for h in range(heads_here):
            at = h * HD % owned
            line[m, k, h * HD // owned, :, at : at + HD] = mixed[
                h * length + k * R : h * length + (k + 1) * R
            ]

    def line_copy(source, j, k, peer):
        block = line.at[source, k]
        return remote(block, block, line_s.at[0], line_r.at[k, j - 1], mp=peer)

    def line_send(k):
        for j in range(1, n):
            line_copy(m, j, k, lax.rem(m + j, n)).start()

    def spread_heads(k):
        for j in range(n):
            source = lax.rem(m + n - j, n)
            if j > 0:
                line_copy(source, j, k, source).wait_recv()
            for i in range(owners):
                owner = source * owners + i

                @pl.when(owner != b)
                def _(source=source, i=i, owner=owner):
                    remote(
                        line.at[source, k, i],
                        rows.at[k, my_slot],
                        owner_s.at[k],
                        owner_r.at[k],
                        batch=owner,
                    ).start()

                @pl.when(owner == b)
                def _(source=source, i=i):
                    rows[k, my_slot] = line[source, k, i]

    def all_owners(k):
        block = rows.at[k, pl.ds(0, nb - 1)]
        return remote(block, block, owner_s.at[k], owner_r.at[k], batch=mate)

    scatter_a = (part_a, near_a, mid_a, far_a, na_s, na_r, fa_s, fa_r)
    scatter_m = (part_m, near_m, mid_m, far_m, nm_s, nm_r, fm_s, fm_r)

    def near_copy(k, bufs):
        part, near, mid, far, near_s, near_r, far_s, far_r = bufs
        block = part.at[k, pl.ds((1 - core) * chips, chips)]
        return remote(block, near.at[k], near_s.at[0], near_r.at[k], batch=mate)

    def scatter_far(k, bufs):
        part, near, mid, far, near_s, near_r, far_s, far_r = bufs
        near_copy(k, bufs).wait_recv()
        for j in range(1, chips):
            target = lax.rem(chip + j, chips)
            mid[k, j - 1] = (
                part[k, core * chips + target].astype(F32) + near[k, target].astype(F32)
            ).astype(BF16)
            remote(
                mid.at[k, j - 1],
                far.at[k, j - 1],
                far_s.at[0],
                far_r.at[k],
                batch=2 * target + core,
            ).start()

    def scatter_total(k, bufs):
        part, near, mid, far, near_s, near_r, far_s, far_r = bufs
        total = part[k, my_slot].astype(F32) + near[k, chip].astype(F32)
        remote(mid.at[k], far.at[k], far_s.at[0], far_r.at[k], batch=mate).wait_recv()
        for j in range(1, chips):
            total = total + far[k, j - 1].astype(F32)
        return total

    tile = 512 if cols_d % 512 == 0 else cols_d
    tiles = cols_d // tile

    def multiply_tile(k, bufs, left, weight, i):
        at = pl.ds(i * tile, tile)
        made = jnp.dot(left, weight[:, at], preferred_element_type=F32).astype(BF16)
        bufs[0][k, :, :, at] = made.reshape(nb, R, tile)
        if i == tiles - 1:
            near_copy(k, bufs).start()

    def swap(k):
        all_owners(k).wait_recv()

        @pl.when(k == 0)
        def _():
            load_wo.wait()

        x = rows[k].reshape(all_rows, owned)
        other = jnp.dot(pmat[...], x, preferred_element_type=F32)
        head = lax.broadcasted_iota(jnp.int32, (all_rows, owned), 1) // HD + b * (owned // HD)
        chosen = head == ablated_ref[0]
        for i in range(1, ablated_ref.shape[0]):
            chosen = chosen | (head == ablated_ref[i])
        swapped[...] = jnp.where(chosen, other, x.astype(F32)).astype(BF16)

    def project(i, k):
        multiply_tile(k, scatter_a, swapped[...], wo_buf, i)

    def rows_at(k):
        return pl.ds(pl.multiple_of(k * R, R), R)

    def out_copy(buf, hbm, k, which):
        return pltpu.make_async_copy(
            buf.at[rows_at(k), :], hbm.at[0, rows_at(k), :], out_sem.at[which]
        )

    def gather_far(k, j, source, peer):
        block = x_all.at[k, core * chips + source]
        return remote(block, block, agf_s.at[0], agf_r.at[k, j - 1], batch=peer)

    def gather_near(k, block):
        return remote(block, block, agn_s.at[0], agn_r.at[k], batch=mate)

    def gather_near_all(k):
        return gather_near(k, x_all.at[k, pl.ds((1 - core) * chips, chips)])

    def square_copy(k):
        place = lax.rem(m + n - end, n) - 1
        return remote(own_sq.at[k], got_sq.at[k, place], sq_s.at[0], sq_r.at[k], mp=end)

    def inverse_wait(k, count):
        block = inv.at[pl.ds(0, count)]
        return remote(block, block, inv_s.at[k], inv_r.at[k], batch=mate)

    def normalize(k):
        total = scatter_total(k, scatter_a)
        attn_buf[rows_at(k), :] = total.astype(BF16)
        out_copy(attn_buf, attn_hbm, k, 0).start()
        state = res_buf[rows_at(k), :].astype(F32) + total
        x_all[k, my_slot] = (state * gain_ref[...].reshape(1, cols_d)).astype(BF16)
        for j in range(1, chips):
            gather_far(k, j, chip, 2 * lax.rem(chip + j, chips) + core).start()
        gather_near(k, x_all.at[k, my_slot]).start()
        squares = jnp.sum(state * state, axis=1, keepdims=True)
        own_sq[k] = jnp.broadcast_to(squares, (R, 128))

        @pl.when(m != end)
        def _():
            square_copy(k).start()

    def gather_rest(k):
        for j in range(1, chips):
            source = lax.rem(chip + chips - j, chips)
            gather_far(k, j, source, mate).wait_recv()
            gather_near(k, x_all.at[k, core * chips + source]).start()

        @pl.when(m == end)
        def _():
            total = own_sq[k]
            remote(got_sq.at[k], got_sq.at[k], sq_s.at[0], sq_r.at[k], mp=end).wait_recv()
            for j in range(1, n):
                total = total + got_sq[k, j - 1]
            mine = k * chips + chip
            inv[mine] = lax.rsqrt(total / D + 1e-05)
            for j in range(1, nb):
                remote(
                    inv.at[mine],
                    inv.at[mine],
                    inv_s.at[k],
                    inv_r.at[k],
                    batch=lax.rem(b + j, nb),
                ).start()

    pos_of = (m, n - 1 - m)
    way_of = (1, -1)

    def sum_copy(d, u, peer):
        at = lax.rem(u, reuse)
        return remote(own.at[d, u], got.at[d, u], sum_s.at[d], sum_r.at[d, at], mp=peer)

    def hid_copy(d, u, peer):
        block = hid.at[d, u]
        at = lax.rem(u, reuse)
        return remote(block, block, hid_s.at[d], hid_r.at[d, at], mp=peer)

    def cut(offset):
        return lax.div(offset, slots), lax.rem(offset, slots)

    made_cut = cut(jnp.int32(LEAD))
    sum_cut = [cut(LEAD + LAG * pos_of[d]) for d in range(2)]
    back_cut = [cut(LEAD + LAG * (n - 1) + HLAG * (n - 1 - pos_of[d])) for d in range(2)]

    def step(window, s):
        def unit(offset):
            q, r = offset
            late = (s < r).astype(jnp.int32)
            k, c = window - q - late, s - r + slots * late
            return k, c, (k >= 0) & (k < chunks) & (c < pieces)

        k, c, here = unit(made_cut)

        @pl.when(here)
        def _():
            @pl.when(c == 0)
            def _():
                gather_near_all(k).wait_recv()

                @pl.when(k == 0)
                def _():
                    pltpu.make_async_copy(w_buf, w_buf, big_sem.at[2]).wait()

            x = x_all[k].reshape(all_rows, cols_d)
            u = k * pieces + c
            if joined:
                made = jnp.dot(x, w_buf[c], preferred_element_type=F32).astype(BF16)
                for d in range(2):
                    own[d, u] = made[d * half : (d + 1) * half]
            else:
                for which in range(2):
                    made = jnp.dot(x, w_buf[c, which], preferred_element_type=F32).astype(BF16)
                    for d in range(2):
                        own[d, u, which] = made[d * half : (d + 1) * half]

        for d in range(2):
            pos, way = pos_of[d], way_of[d]
            k, c, here = unit(sum_cut[d])
            u = k * pieces + c

            @pl.when(here & (pos == 0))
            def _(d=d, u=u, way=way):
                sum_copy(d, u, m + way).start()

            @pl.when(here & (pos > 0) & (pos < n - 1))
            def _(d=d, u=u, way=way):
                sum_copy(d, u, m - way).wait_recv()
                own[d, u] = (own[d, u].astype(F32) + got[d, u].astype(F32)).astype(BF16)
                sum_copy(d, u, m + way).start()

            @pl.when(here & (pos == n - 1))
            def _(d=d, k=k, c=c, u=u, way=way):
                @pl.when(c == 0)
                def _():
                    @pl.when(core == d)
                    def _():
                        inverse_wait(k, chips - 1).wait_recv()

                    @pl.when(core != d)
                    def _():
                        inverse_wait(k, chips).wait_recv()

                sum_copy(d, u, m - way).wait_recv()
                inverse = inv[pl.ds(k * chips, chips)].reshape(half, 128)[:, :1]
                summed = own[d, u].astype(F32) + got[d, u].astype(F32)
                gate = (summed[:, :w] if joined else summed[0]) * inverse
                up = (summed[:, w:] if joined else summed[1]) * inverse
                hid[d, u] = (gate / (1.0 + jnp.exp(-gate)) * up).astype(BF16)
                hid_copy(d, u, m - way).start()

            k, c, here = unit(back_cut[d])
            u = k * pieces + c

            @pl.when(here & (pos < n - 1))
            def _(d=d, u=u, way=way, pos=pos):
                hid_copy(d, u, m + way).wait_recv()

                @pl.when(pos > 0)
                def _():
                    hid_copy(d, u, m - way).start()

        def stage(offset, first, do):
            q, r = divmod(LEAD + offset, slots)
            k = window - q

            @pl.when((s == r) & (k >= first) & (k < chunks))
            def _():
                do(k)

        def start_scatter(k):
            scatter_far(k, scatter_a)

            @pl.when(k == 0)
            def _():
                for later in range(2, chunks):
                    line_send(later)

        def down(i, k):
            if i == 0:

                @pl.when(k == 0)
                def _():
                    load_wd.wait()

            left = [
                jnp.concatenate([hid[d, k * pieces + c] for c in range(pieces)], axis=1)
                for d in range(2)
            ]
            multiply_tile(k, scatter_m, jnp.concatenate(left, axis=0), wd_buf, i)

        def finish_rows(k):
            mlp_buf[rows_at(k), :] = scatter_total(k, scatter_m).astype(BF16)
            out_copy(mlp_buf, mlp_hbm, k, 1).start()

        for i in range(tiles):
            stage(done + i, 0, functools.partial(down, i))
        stage(done + tiles + 1, 0, lambda k: scatter_far(k, scatter_m))
        stage(done + FINISH, 0, finish_rows)
        stage(-LEAD, 0, swap)
        for i in range(tiles):
            stage(-LEAD + (i * 4) // tiles, 0, functools.partial(project, i))
        stage(-15, 0, start_scatter)
        stage(-26, 1, spread_heads)
        stage(-8, 0, normalize)
        stage(-3, 0, gather_rest)

    done = pieces - 1 + LAG * (n - 1) + HLAG * (n - 1)
    pl.semaphore_wait(barrier, n + nb - 2)
    line_send(0)
    spread_heads(0)
    if chunks > 1:
        line_send(1)
    small[3].wait()
    last = LEAD + (chunks - 1) * slots + done + FINISH + 1

    def window_steps(window, carry):
        def one(s, carry):
            step(window, s)
            return carry

        return lax.fori_loop(0, slots, one, carry)

    lax.fori_loop(0, -(-last // slots), window_steps, 0)

    pltpu.make_async_copy(attn_buf, attn_hbm.at[0], out_sem.at[0]).wait()
    pltpu.make_async_copy(mlp_buf, mlp_hbm.at[0], out_sem.at[1]).wait()
    block = line.at[pl.ds(0, n - 1)]
    remote(block, block, line_s.at[0], line_r.at[0, 0], mp=end).wait_send()
    for k in range(chunks):
        all_owners(k).wait_send()
    for part, near, mid, far, near_s, near_r, far_s, far_r in (scatter_a, scatter_m):
        remote(near, near, near_s.at[0], near_r.at[0], batch=mate).wait_send()
        remote(mid, mid, far_s.at[0], far_r.at[0], batch=mate).wait_send()
    remote(mid_a, mid_a, agf_s.at[0], agf_r.at[0, 0], batch=mate).wait_send()
    remote(near_a, near_a, agn_s.at[0], agn_r.at[0], batch=mate).wait_send()

    @pl.when(m != end)
    def _():
        remote(own_sq, own_sq, sq_s.at[0], sq_r.at[0], mp=end).wait_send()

    @pl.when(m == end)
    def _():
        for k in range(chunks):
            inverse_wait(k, nb - 1).wait_send()

    for d in range(2):
        pos, way = pos_of[d], way_of[d]

        @pl.when(pos < n - 1)
        def _(d=d, way=way):
            remote(own.at[d], got.at[d], sum_s.at[d], sum_r.at[d, 0], mp=m + way).wait_send()

        @pl.when(pos > 0)
        def _(d=d, way=way):
            remote(hid.at[d], hid.at[d], hid_s.at[d], hid_r.at[d, 0], mp=m - way).wait_send()


def body(
    residual, query_states, key_states, value_states, prompt_perm, ablated_heads, out_weight,
    rms_gain, gate_weight, up_weight, down_weight,
):
    _, length, cols_d = residual.shape
    nb, n = lax.axis_size("batch"), lax.axis_size("mp")
    chips = nb // 2
    chunks = length // R
    owned = out_weight.shape[0]
    columns = query_states.shape[2]
    owners = columns // owned
    width = gate_weight.shape[1]
    joined = width % 128 == 0
    w = 128 if joined else width
    pieces = width // w
    slots = max(pieces, 14)
    units = chunks * pieces
    reuse = min(units, (LAG + HLAG) * (n - 1) + 1)
    half = chips * R
    pair = (half, 2 * w) if joined else (2, half, w)
    vmem = pl.BlockSpec(memory_space=pltpu.VMEM)
    smem = pl.BlockSpec(memory_space=pltpu.SMEM)
    anywhere = pl.BlockSpec(memory_space=pl.ANY)
    dma = pltpu.SemaphoreType.DMA

    def scatter_bufs():
        return [
            pltpu.VMEM((chunks, nb, R, cols_d), BF16),
            pltpu.VMEM((chunks, chips, R, cols_d), BF16),
            pltpu.VMEM((chunks, chips - 1, R, cols_d), BF16),
            pltpu.VMEM((chunks, chips - 1, R, cols_d), BF16),
        ]

    out = jax.ShapeDtypeStruct((1, length, cols_d), BF16)
    attn, mlp = pl.pallas_call(
        functools.partial(layer_kernel, nb, n, slots, w, joined),
        in_specs=[smem, smem] + [anywhere] * 5 + [vmem] + [anywhere] * 3,
        out_specs=[anywhere, anywhere],
        out_shape=[out, out],
        scratch_shapes=[
            pltpu.VMEM((length, cols_d), BF16),
            pltpu.VMEM((length, cols_d), BF16),
            pltpu.VMEM((length, cols_d), BF16),
            pltpu.VMEM((length, columns), BF16),
            pltpu.VMEM((length, HD), BF16),
            pltpu.VMEM((length, HD), BF16),
            pltpu.VMEM((owned, cols_d), BF16),
            pltpu.VMEM((pieces, cols_d, 2 * w) if joined else (pieces, 2, cols_d, w), BF16),
            pltpu.VMEM((width, cols_d), BF16),
            pltpu.VMEM((nb * R, nb * R), BF16),
            pltpu.VMEM((n, chunks, owners, R, owned), BF16),
            pltpu.VMEM((chunks, nb, R, owned), BF16),
            pltpu.VMEM((nb * R, owned), BF16),
            *scatter_bufs(),
            *scatter_bufs(),
            pltpu.VMEM((chunks, nb, R, cols_d), BF16),
            pltpu.VMEM((chunks, R, 128), F32),
            pltpu.VMEM((chunks, n - 1, R, 128), F32),
            pltpu.VMEM((chunks * chips, R, 128), F32),
            pltpu.VMEM((2, units, *pair), BF16),
            pltpu.VMEM((2, units, *pair), BF16),
            pltpu.VMEM((2, units, half, w), BF16),
            dma((4,)),
            dma((3,)),
            dma((2,)),
            dma((1,)),
            dma((chunks, n - 1)),
            dma((chunks,)),
            dma((chunks,)),
            *[dma((1,)), dma((chunks,)), dma((1,)), dma((chunks,))] * 2,
            dma((1,)),
            dma((chunks, chips - 1)),
            dma((1,)),
            dma((chunks,)),
            dma((1,)),
            dma((chunks,)),
            dma((chunks,)),
            dma((chunks,)),
            dma((2,)),
            dma((2, reuse)),
            dma((2,)),
            dma((2, reuse)),
        ],
        compiler_params=pltpu.CompilerParams(
            collective_id=1, has_side_effects=True, vmem_limit_bytes=VMEM
        ),
    )(
        prompt_perm, ablated_heads, residual, query_states, key_states, value_states, out_weight,
        rms_gain, gate_weight, up_weight, down_weight,
    )
    return pl.pallas_call(
        place_kernel,
        in_specs=[anywhere, anywhere],
        out_specs=[anywhere, anywhere],
        out_shape=[out, out],
        scratch_shapes=[pltpu.VMEM(out.shape, BF16), pltpu.VMEM(out.shape, BF16), dma((2, 2, 2))],
    )(attn, mlp)


def place_kernel(attn_ref, mlp_ref, attn_out, mlp_out, attn_buf, mlp_buf, sem):
    rows = attn_ref.shape[1] // 2
    pairs = ((attn_ref, attn_buf, attn_out), (mlp_ref, mlp_buf, mlp_out))
    moves = [(i, j, pl.ds(j * rows, rows)) for j in range(2) for i in range(2)]

    def load(i, j, at):
        src, buf, dst = pairs[i]
        return pltpu.make_async_copy(src.at[:, at], buf.at[:, at], sem.at[0, i, j])

    def store(i, j, at):
        src, buf, dst = pairs[i]
        return pltpu.make_async_copy(buf.at[:, at], dst.at[:, at], sem.at[1, i, j])

    for move in moves:
        load(*move).start()
    for move in moves:
        load(*move).wait()
        store(*move).start()
    for move in moves:
        store(*move).wait()


def solution(mesh):
    placed = (
        P("batch", None, "mp"),
        P("batch", None, "mp"),
        P("batch", None, None),
        P("batch", None, None),
        P(),
        P(),
        P("batch", "mp"),
        P("mp"),
        P("mp", "batch"),
        P("mp", "batch"),
        P("batch", "mp"),
    )
    return jax.shard_map(
        body,
        mesh=mesh,
        in_specs=placed,
        out_specs=(P("batch", None, "mp"), P("batch", None, "mp")),
        check_vma=False,
    )
```

```python
import functools
import math

import jax
import jax.numpy as jnp
from jax import lax
from jax.experimental import pallas as pl
from jax.experimental.pallas import tpu as pltpu
from jax.sharding import PartitionSpec as P

D = 8192
HEADS = 32
KV = 4
HD = 128
R = 16
LAG = 4
HLAG = 4
LEAD = 20
FINISH = 12
DIRECT = 6
VMEM = 60 * 2**20
BF16, F32 = jnp.bfloat16, jnp.float32


def remote(src, dst, send_sem, recv_sem, **peer):
    return pltpu.make_async_remote_copy(
        src_ref=src,
        dst_ref=dst,
        send_sem=send_sem,
        recv_sem=recv_sem,
        device_id=peer,
        device_id_type=pl.DeviceIdType.MESH,
    )


def layer_kernel(
    nb, n, slots, w, joined,
    perm_ref, ablated_ref, res_hbm, q_hbm, k_hbm, v_hbm, wo_hbm, gain_ref, wg_hbm, wu_hbm, wd_hbm,
    attn_hbm, mlp_hbm,
    attn_buf, mlp_buf, res_buf, q_buf, k_buf, v_buf, wo_buf, w_buf, wd_buf,
    pmat, line, rows, swapped,
    part_a, near_a, mid_a, far_a, part_m, near_m, mid_m, far_m,
    x_all, own_sq, got_sq, inv, own, got, hid,
    small_sem, big_sem, out_sem,
    line_s, line_r, owner_s, owner_r,
    na_s, na_r, fa_s, fa_r, nm_s, nm_r, fm_s, fm_r,
    agf_s, agf_r, agn_s, agn_r, sq_s, sq_r, inv_s, inv_r, sum_s, sum_r, hid_s, hid_r,
):
    b, m = lax.axis_index("batch"), lax.axis_index("mp")
    chips = nb // 2
    core, chip = lax.rem(b, 2), lax.div(b, 2)
    mate = b + 1 - 2 * core
    my_slot = core * chips + chip
    length, cols_d = res_buf.shape
    chunks = length // R
    _, _, owners, _, owned = line.shape
    pieces = w_buf.shape[0]
    reuse = sum_r.shape[1]
    units = chunks * pieces
    direct = min(DIRECT, units // (n - 1))
    half = chips * R
    all_rows = nb * R
    heads_here = q_buf.shape[1] // HD
    end = (n - 1) * (1 - core)

    def slot_of(device):
        return lax.rem(device, 2) * chips + lax.div(device, 2)

    kv = lax.div(m * heads_here, HEADS // KV)
    kv = pl.ds(pl.multiple_of(kv * HD, HD), HD)
    small = [
        pltpu.make_async_copy(src, dst, small_sem.at[i])
        for i, (src, dst) in enumerate(
            (
                (q_hbm.at[0], q_buf),
                (k_hbm.at[0, :, kv], k_buf),
                (v_hbm.at[0, :, kv], v_buf),
                (res_hbm.at[0], res_buf),
            )
        )
    ]
    load_wo = pltpu.make_async_copy(wo_hbm, wo_buf, big_sem.at[0])
    load_wd = pltpu.make_async_copy(wd_hbm, wd_buf, big_sem.at[1])

    def piece(c):
        return pl.ds(0, w) if pieces == 1 else pl.ds(pl.multiple_of(c * w, w), w)

    for copy in small:
        copy.start()
    barrier = pltpu.get_barrier_semaphore()
    for axis, at, size in (("mp", m, n), ("batch", b, nb)):
        for k in range(1, size):
            pl.semaphore_signal(
                barrier,
                inc=1,
                device_id={axis: lax.rem(at + k, size)},
                device_id_type=pl.DeviceIdType.MESH,
            )
    load_wo.start()
    for c in range(pieces):
        for i, src in enumerate((wg_hbm, wu_hbm)):
            dst = w_buf.at[c, :, pl.ds(i * w, w)] if joined else w_buf.at[c, i]
            pltpu.make_async_copy(src.at[:, piece(c)], dst, big_sem.at[2]).start()
    load_wd.start()

    at_row = lax.broadcasted_iota(jnp.int32, (R, all_rows), 0)
    at_col = lax.broadcasted_iota(jnp.int32, (R, all_rows), 1)
    for slot in range(nb):
        source = slot_of(perm_ref[2 * (slot % chips) + slot // chips])
        hit = at_col - at_row == source * R
        pmat[slot * R : (slot + 1) * R, :] = jnp.where(hit, 1.0, 0.0).astype(BF16)

    for copy in small[:3]:
        copy.wait()
    q = jnp.concatenate([q_buf[:, h * HD : (h + 1) * HD] for h in range(heads_here)], axis=0)
    scores = lax.dot_general(
        q, k_buf[...], (((1,), (1,)), ((), ())), preferred_element_type=F32
    ) / math.sqrt(HD)
    position = lax.rem(lax.broadcasted_iota(jnp.int32, scores.shape, 0), length)
    causal = position >= lax.broadcasted_iota(jnp.int32, scores.shape, 1)
    scores = jnp.where(causal, scores, -1e30)
    weights = jnp.exp(scores - jnp.max(scores, axis=-1, keepdims=True))
    probability = weights / jnp.sum(weights, axis=-1, keepdims=True)
    mixed = jnp.dot(probability.astype(BF16), v_buf[...], preferred_element_type=F32).astype(BF16)
    for k in range(chunks):
        for h in range(heads_here):
            at = h * HD % owned
            line[m, k, h * HD // owned, :, at : at + HD] = mixed[
                h * length + k * R : h * length + (k + 1) * R
            ]

    def line_copy(source, j, k, peer):
        block = line.at[source, k]
        return remote(block, block, line_s.at[0], line_r.at[k, j - 1], mp=peer)

    def line_send(k):
        for j in range(1, n):
            line_copy(m, j, k, lax.rem(m + j, n)).start()

    def spread_heads(k):
        for j in range(n):
            source = lax.rem(m + n - j, n)
            if j > 0:
                line_copy(source, j, k, source).wait_recv()
            for i in range(owners):
                owner = source * owners + i

                @pl.when(owner != b)
                def _(source=source, i=i, owner=owner):
                    remote(
                        line.at[source, k, i],
                        rows.at[k, my_slot],
                        owner_s.at[k],
                        owner_r.at[k],
                        batch=owner,
                    ).start()

                @pl.when(owner == b)
                def _(source=source, i=i):
                    rows[k, my_slot] = line[source, k, i]

    def all_owners(k):
        block = rows.at[k, pl.ds(0, nb - 1)]
        return remote(block, block, owner_s.at[k], owner_r.at[k], batch=mate)

    scatter_a = (part_a, near_a, mid_a, far_a, na_s, na_r, fa_s, fa_r)
    scatter_m = (part_m, near_m, mid_m, far_m, nm_s, nm_r, fm_s, fm_r)

    part_cols = [pl.ds(h * cols_d // 2, cols_d // 2) for h in range(2)]

    def near_copy(k, h, bufs):
        part, near, mid, far, near_s, near_r, far_s, far_r = bufs
        block = part.at[k, pl.ds((1 - core) * chips, chips), :, part_cols[h]]
        return remote(
            block, near.at[k, :, :, part_cols[h]], near_s.at[0], near_r.at[k, h], batch=mate
        )

    def scatter_far(h, bufs, k):
        part, near, mid, far, near_s, near_r, far_s, far_r = bufs
        near_copy(k, h, bufs).wait_recv()
        at = part_cols[h]
        for j in range(1, chips):
            target = lax.rem(chip + j, chips)
            mid[k, j - 1, :, at] = (
                part[k, core * chips + target, :, at].astype(F32)
                + near[k, target, :, at].astype(F32)
            ).astype(BF16)
            remote(
                mid.at[k, j - 1, :, at],
                far.at[k, j - 1, :, at],
                far_s.at[0],
                far_r.at[k, h],
                batch=2 * target + core,
            ).start()

    def scatter_total(k, h, bufs):
        part, near, mid, far, near_s, near_r, far_s, far_r = bufs
        at = part_cols[h]
        total = part[k, my_slot, :, at].astype(F32) + near[k, chip, :, at].astype(F32)
        remote(
            mid.at[k, :, :, at], far.at[k, :, :, at], far_s.at[0], far_r.at[k, h], batch=mate
        ).wait_recv()
        for j in range(1, chips):
            total = total + far[k, j - 1, :, at].astype(F32)
        return total

    tile = 512 if cols_d % 1024 == 0 else cols_d // 2
    tiles = cols_d // tile // 2

    def multiply_half(k, h, bufs, left, weight):
        for i in range(h * tiles, (h + 1) * tiles):
            at = pl.ds(i * tile, tile)
            made = jnp.dot(left, weight[:, at], preferred_element_type=F32).astype(BF16)
            bufs[0][k, :, :, at] = made.reshape(nb, R, tile)
        near_copy(k, h, bufs).start()

    def swap(k):
        all_owners(k).wait_recv()

        @pl.when(k == 0)
        def _():
            load_wo.wait()

        x = rows[k].reshape(all_rows, owned)
        other = jnp.dot(pmat[...], x, preferred_element_type=F32)
        head = lax.broadcasted_iota(jnp.int32, (all_rows, owned), 1) // HD + b * (owned // HD)
        chosen = head == ablated_ref[0]
        for i in range(1, ablated_ref.shape[0]):
            chosen = chosen | (head == ablated_ref[i])
        swapped[...] = jnp.where(chosen, other, x.astype(F32)).astype(BF16)

    def project(h, k):
        multiply_half(k, h, scatter_a, swapped[...], wo_buf)

    def rows_at(k):
        return pl.ds(pl.multiple_of(k * R, R), R)

    def out_copy(buf, hbm, k, which):
        return pltpu.make_async_copy(
            buf.at[rows_at(k), :], hbm.at[0, rows_at(k), :], out_sem.at[which]
        )

    def gather_far(k, h, j, source, peer):
        block = x_all.at[k, core * chips + source, :, part_cols[h]]
        return remote(block, block, agf_s.at[0], agf_r.at[k, j - 1, h], batch=peer)

    def gather_near(k, h, slots):
        block = x_all.at[k, slots, :, part_cols[h]]
        return remote(block, block, agn_s.at[0], agn_r.at[k, h], batch=mate)

    def square_copy(k):
        place = lax.rem(m + n - end, n) - 1
        return remote(own_sq.at[k], got_sq.at[k, place], sq_s.at[0], sq_r.at[k], mp=end)

    def inverse_wait(k, count):
        block = inv.at[pl.ds(0, count)]
        return remote(block, block, inv_s.at[k], inv_r.at[k], batch=mate)

    def normalize(h, k):
        at = part_cols[h]
        total = scatter_total(k, h, scatter_a)
        attn_buf[rows_at(k), at] = total.astype(BF16)
        state = res_buf[rows_at(k), at].astype(F32) + total
        x_all[k, my_slot, :, at] = (state * gain_ref[at].reshape(1, cols_d // 2)).astype(BF16)
        for j in range(1, chips):
            gather_far(k, h, j, chip, 2 * lax.rem(chip + j, chips) + core).start()
        gather_near(k, h, my_slot).start()
        squares = jnp.broadcast_to(jnp.sum(state * state, axis=1, keepdims=True), (R, 128))
        if h == 0:
            own_sq[k] = squares
            return
        own_sq[k] = own_sq[k] + squares
        out_copy(attn_buf, attn_hbm, k, 0).start()

        @pl.when(m != end)
        def _():
            square_copy(k).start()

    def gather_rest(h, k):
        for j in range(1, chips):
            source = lax.rem(chip + chips - j, chips)
            gather_far(k, h, j, source, mate).wait_recv()
            gather_near(k, h, core * chips + source).start()
        if h == 0:
            return

        @pl.when(m == end)
        def _():
            total = own_sq[k]
            remote(got_sq.at[k], got_sq.at[k], sq_s.at[0], sq_r.at[k], mp=end).wait_recv()
            for j in range(1, n):
                total = total + got_sq[k, j - 1]
            mine = k * chips + chip
            inv[mine] = lax.rsqrt(total / D + 1e-05)
            for j in range(1, nb):
                remote(
                    inv.at[mine],
                    inv.at[mine],
                    inv_s.at[k],
                    inv_r.at[k],
                    batch=lax.rem(b + j, nb),
                ).start()

    pos_of = (m, n - 1 - m)
    way_of = (1, -1)

    def sum_copy(d, u, peer):
        at = lax.rem(u, reuse)
        return remote(own.at[d, u], got.at[d, u], sum_s.at[d], sum_r.at[d, at], mp=peer)

    def hid_copy(d, u, peer):
        block = hid.at[d, u]
        at = lax.rem(u, reuse)
        return remote(block, block, hid_s.at[d], hid_r.at[d, at], mp=peer)

    def hid_direct(d, u, peer):
        block = hid.at[d, u]
        at = lax.rem(u, reuse)
        return remote(block, block, hid_s.at[2 + d], hid_r.at[d, at], mp=peer)

    def cut(offset):
        return lax.div(offset, slots), lax.rem(offset, slots)

    made_cut = cut(jnp.int32(LEAD))
    sum_cut = [cut(LEAD + LAG * pos_of[d]) for d in range(2)]
    back_cut = [cut(LEAD + LAG * (n - 1) + HLAG * (n - 1 - pos_of[d])) for d in range(2)]

    def step(window, s):
        def unit(offset):
            q, r = offset
            late = (s < r).astype(jnp.int32)
            k, c = window - q - late, s - r + slots * late
            return k, c, (k >= 0) & (k < chunks) & (c < pieces)

        k, c, here = unit(made_cut)

        @pl.when(here)
        def _():
            @pl.when(c == 0)
            def _():
                for h in range(2):
                    gather_near(k, h, pl.ds((1 - core) * chips, chips)).wait_recv()

                @pl.when(k == 0)
                def _():
                    pltpu.make_async_copy(w_buf, w_buf, big_sem.at[2]).wait()

            x = x_all[k].reshape(all_rows, cols_d)
            u = k * pieces + c
            if joined:
                made = jnp.dot(x, w_buf[c], preferred_element_type=F32).astype(BF16)
                for d in range(2):
                    own[d, u] = made[d * half : (d + 1) * half]
            else:
                for which in range(2):
                    made = jnp.dot(x, w_buf[c, which], preferred_element_type=F32).astype(BF16)
                    for d in range(2):
                        own[d, u, which] = made[d * half : (d + 1) * half]

        for d in range(2):
            pos, way = pos_of[d], way_of[d]
            k, c, here = unit(sum_cut[d])
            u = k * pieces + c

            @pl.when(here & (pos == 0))
            def _(d=d, u=u, way=way):
                sum_copy(d, u, m + way).start()

            @pl.when(here & (pos > 0) & (pos < n - 1))
            def _(d=d, u=u, way=way):
                sum_copy(d, u, m - way).wait_recv()
                own[d, u] = (own[d, u].astype(F32) + got[d, u].astype(F32)).astype(BF16)
                sum_copy(d, u, m + way).start()

            @pl.when(here & (pos == n - 1))
            def _(d=d, k=k, c=c, u=u, way=way):
                @pl.when(c == 0)
                def _():
                    @pl.when(core == d)
                    def _():
                        inverse_wait(k, chips - 1).wait_recv()

                    @pl.when(core != d)
                    def _():
                        inverse_wait(k, chips).wait_recv()

                sum_copy(d, u, m - way).wait_recv()
                inverse = inv[pl.ds(k * chips, chips)].reshape(half, 128)[:, :1]
                summed = own[d, u].astype(F32) + got[d, u].astype(F32)
                gate = (summed[:, :w] if joined else summed[0]) * inverse
                up = (summed[:, w:] if joined else summed[1]) * inverse
                hid[d, u] = (gate / (1.0 + jnp.exp(-gate)) * up).astype(BF16)

                @pl.when(u < units - direct)
                def _():
                    hid_copy(d, u, m - way).start()

                @pl.when(u >= units - direct)
                def _():
                    for j in range(1, n):
                        hid_direct(d, u, m - way * j).start()

            k, c, here = unit(back_cut[d])
            u = k * pieces + c

            @pl.when(here & (pos < n - 1))
            def _(d=d, u=u, way=way, pos=pos):
                hid_copy(d, u, m + way).wait_recv()

                @pl.when((pos > 0) & (u < units - direct))
                def _():
                    hid_copy(d, u, m - way).start()

        def stage(offset, first, do):
            q, r = divmod(LEAD + offset, slots)
            k = window - q

            @pl.when((s == r) & (k >= first) & (k < chunks))
            def _():
                do(k)

        def start_scatter(k):
            scatter_far(1, scatter_a, k)

            @pl.when(k == 0)
            def _():
                for later in range(2, chunks):
                    line_send(later)

        def down(h, k):
            if h == 0:

                @pl.when(k == 0)
                def _():
                    load_wd.wait()

            left = [
                jnp.concatenate([hid[d, k * pieces + c] for c in range(pieces)], axis=1)
                for d in range(2)
            ]
            multiply_half(k, h, scatter_m, jnp.concatenate(left, axis=0), wd_buf)

        def finish_rows(h, k):
            mlp_buf[rows_at(k), part_cols[h]] = scatter_total(k, h, scatter_m).astype(BF16)
            if h == 1:
                out_copy(mlp_buf, mlp_hbm, k, 1).start()

        for h in range(2):
            stage(done + h, 0, functools.partial(down, h))
        for h in range(2):
            stage(done + 2 + h, 0, functools.partial(scatter_far, h, scatter_m))
        for h in range(2):
            stage(done + FINISH - 1 + h, 0, functools.partial(finish_rows, h))
        stage(-LEAD, 0, swap)
        for h in range(2):
            stage(-LEAD + h, 0, functools.partial(project, h))
        stage(-17, 0, functools.partial(scatter_far, 0, scatter_a))
        stage(-16, 0, start_scatter)
        stage(-26, 1, spread_heads)
        for h in range(2):
            stage(-8 + h, 0, functools.partial(normalize, h))
        for h in range(2):
            stage(-2 + h, 0, functools.partial(gather_rest, h))

    done = pieces - 1 + LAG * (n - 1) + HLAG * (n - 1)
    pl.semaphore_wait(barrier, n + nb - 2)
    line_send(0)
    spread_heads(0)
    if chunks > 1:
        line_send(1)
    small[3].wait()
    last = LEAD + (chunks - 1) * slots + done + FINISH + 1

    def window_steps(window, carry):
        def one(s, carry):
            step(window, s)
            return carry

        return lax.fori_loop(0, slots, one, carry)

    lax.fori_loop(0, -(-last // slots), window_steps, 0)

    pltpu.make_async_copy(attn_buf, attn_hbm.at[0], out_sem.at[0]).wait()
    pltpu.make_async_copy(mlp_buf, mlp_hbm.at[0], out_sem.at[1]).wait()
    block = line.at[pl.ds(0, n - 1)]
    remote(block, block, line_s.at[0], line_r.at[0, 0], mp=end).wait_send()
    for k in range(chunks):
        all_owners(k).wait_send()
    for part, near, mid, far, near_s, near_r, far_s, far_r in (scatter_a, scatter_m):
        remote(near, near, near_s.at[0], near_r.at[0, 0], batch=mate).wait_send()
        remote(mid, mid, far_s.at[0], far_r.at[0, 0], batch=mate).wait_send()
    remote(mid_a, mid_a, agf_s.at[0], agf_r.at[0, 0, 0], batch=mate).wait_send()
    remote(near_a, near_a, agn_s.at[0], agn_r.at[0, 0], batch=mate).wait_send()

    @pl.when(m != end)
    def _():
        remote(own_sq, own_sq, sq_s.at[0], sq_r.at[0], mp=end).wait_send()

    @pl.when(m == end)
    def _():
        for k in range(chunks):
            inverse_wait(k, nb - 1).wait_send()

    for d in range(2):
        pos, way = pos_of[d], way_of[d]

        @pl.when(pos < n - 1)
        def _(d=d, way=way):
            remote(own.at[d], got.at[d], sum_s.at[d], sum_r.at[d, 0], mp=m + way).wait_send()

        @pl.when(pos > 0)
        def _(d=d, way=way):
            block = hid.at[d, pl.ds(0, units - direct)]
            remote(block, block, hid_s.at[d], hid_r.at[d, 0], mp=m - way).wait_send()

        if direct:

            @pl.when(pos == n - 1)
            def _(d=d, way=way):
                block = hid.at[d, pl.ds(0, direct * (n - 1))]
                remote(block, block, hid_s.at[2 + d], hid_r.at[d, 0], mp=m - way).wait_send()


def body(
    residual, query_states, key_states, value_states, prompt_perm, ablated_heads, out_weight,
    rms_gain, gate_weight, up_weight, down_weight,
):
    _, length, cols_d = residual.shape
    nb, n = lax.axis_size("batch"), lax.axis_size("mp")
    chips = nb // 2
    chunks = length // R
    owned = out_weight.shape[0]
    columns = query_states.shape[2]
    owners = columns // owned
    width = gate_weight.shape[1]
    joined = width % 128 == 0
    w = 128 if joined else width
    pieces = width // w
    slots = max(pieces, 14)
    units = chunks * pieces
    reuse = min(units, (LAG + HLAG) * (n - 1) + 1)
    half = chips * R
    pair = (half, 2 * w) if joined else (2, half, w)
    vmem = pl.BlockSpec(memory_space=pltpu.VMEM)
    smem = pl.BlockSpec(memory_space=pltpu.SMEM)
    anywhere = pl.BlockSpec(memory_space=pl.ANY)
    dma = pltpu.SemaphoreType.DMA

    def scatter_bufs():
        return [
            pltpu.VMEM((chunks, nb, R, cols_d), BF16),
            pltpu.VMEM((chunks, chips, R, cols_d), BF16),
            pltpu.VMEM((chunks, chips - 1, R, cols_d), BF16),
            pltpu.VMEM((chunks, chips - 1, R, cols_d), BF16),
        ]

    out = jax.ShapeDtypeStruct((1, length, cols_d), BF16)
    attn, mlp = pl.pallas_call(
        functools.partial(layer_kernel, nb, n, slots, w, joined),
        in_specs=[smem, smem] + [anywhere] * 5 + [vmem] + [anywhere] * 3,
        out_specs=[anywhere, anywhere],
        out_shape=[out, out],
        scratch_shapes=[
            pltpu.VMEM((length, cols_d), BF16),
            pltpu.VMEM((length, cols_d), BF16),
            pltpu.VMEM((length, cols_d), BF16),
            pltpu.VMEM((length, columns), BF16),
            pltpu.VMEM((length, HD), BF16),
            pltpu.VMEM((length, HD), BF16),
            pltpu.VMEM((owned, cols_d), BF16),
            pltpu.VMEM((pieces, cols_d, 2 * w) if joined else (pieces, 2, cols_d, w), BF16),
            pltpu.VMEM((width, cols_d), BF16),
            pltpu.VMEM((nb * R, nb * R), BF16),
            pltpu.VMEM((n, chunks, owners, R, owned), BF16),
            pltpu.VMEM((chunks, nb, R, owned), BF16),
            pltpu.VMEM((nb * R, owned), BF16),
            *scatter_bufs(),
            *scatter_bufs(),
            pltpu.VMEM((chunks, nb, R, cols_d), BF16),
            pltpu.VMEM((chunks, R, 128), F32),
            pltpu.VMEM((chunks, n - 1, R, 128), F32),
            pltpu.VMEM((chunks * chips, R, 128), F32),
            pltpu.VMEM((2, units, *pair), BF16),
            pltpu.VMEM((2, units, *pair), BF16),
            pltpu.VMEM((2, units, half, w), BF16),
            dma((4,)),
            dma((3,)),
            dma((2,)),
            dma((1,)),
            dma((chunks, n - 1)),
            dma((chunks,)),
            dma((chunks,)),
            *[dma((1,)), dma((chunks, 2))] * 4,
            dma((1,)),
            dma((chunks, chips - 1, 2)),
            dma((1,)),
            dma((chunks, 2)),
            dma((1,)),
            dma((chunks,)),
            dma((chunks,)),
            dma((chunks,)),
            dma((2,)),
            dma((2, reuse)),
            dma((4,)),
            dma((2, reuse)),
        ],
        compiler_params=pltpu.CompilerParams(
            collective_id=1, has_side_effects=True, vmem_limit_bytes=VMEM
        ),
    )(
        prompt_perm, ablated_heads, residual, query_states, key_states, value_states, out_weight,
        rms_gain, gate_weight, up_weight, down_weight,
    )
    return pl.pallas_call(
        place_kernel,
        in_specs=[anywhere, anywhere],
        out_specs=[anywhere, anywhere],
        out_shape=[out, out],
        scratch_shapes=[pltpu.VMEM(out.shape, BF16), pltpu.VMEM(out.shape, BF16), dma((2, 2, 2))],
    )(attn, mlp)


def place_kernel(attn_ref, mlp_ref, attn_out, mlp_out, attn_buf, mlp_buf, sem):
    rows = attn_ref.shape[1] // 2
    pairs = ((attn_ref, attn_buf, attn_out), (mlp_ref, mlp_buf, mlp_out))
    moves = [(i, j, pl.ds(j * rows, rows)) for j in range(2) for i in range(2)]

    def load(i, j, at):
        src, buf, dst = pairs[i]
        return pltpu.make_async_copy(src.at[:, at], buf.at[:, at], sem.at[0, i, j])

    def store(i, j, at):
        src, buf, dst = pairs[i]
        return pltpu.make_async_copy(buf.at[:, at], dst.at[:, at], sem.at[1, i, j])

    for move in moves:
        load(*move).start()
    for move in moves:
        load(*move).wait()
        store(*move).start()
    for move in moves:
        store(*move).wait()


def solution(mesh):
    placed = (
        P("batch", None, "mp"),
        P("batch", None, "mp"),
        P("batch", None, None),
        P("batch", None, None),
        P(),
        P(),
        P("batch", "mp"),
        P("mp"),
        P("mp", "batch"),
        P("mp", "batch"),
        P("batch", "mp"),
    )
    return jax.shard_map(
        body,
        mesh=mesh,
        in_specs=placed,
        out_specs=(P("batch", None, "mp"), P("batch", None, "mp")),
        check_vma=False,
    )
```

```python
import functools
import math

import jax
import jax.numpy as jnp
from jax import lax
from jax.experimental import pallas as pl
from jax.experimental.pallas import tpu as pltpu
from jax.sharding import PartitionSpec as P

D = 8192
HEADS = 32
KV = 4
HD = 128
R = 16
LAG = 4
HLAG = 4
LEAD = 20
FINISH = 12
DIRECT = 3
VMEM = 60 * 2**20
BF16, F32 = jnp.bfloat16, jnp.float32


def remote(src, dst, send_sem, recv_sem, **peer):
    return pltpu.make_async_remote_copy(
        src_ref=src,
        dst_ref=dst,
        send_sem=send_sem,
        recv_sem=recv_sem,
        device_id=peer,
        device_id_type=pl.DeviceIdType.MESH,
    )


def layer_kernel(
    nb, n, slots, w, joined,
    perm_ref, ablated_ref, res_hbm, q_hbm, k_hbm, v_hbm, wo_hbm, gain_ref, wg_hbm, wu_hbm, wd_hbm,
    attn_hbm, mlp_hbm,
    attn_buf, mlp_buf, res_buf, q_buf, k_buf, v_buf, wo_buf, w_buf, wd_buf,
    pmat, line, rows, swapped,
    part_a, near_a, mid_a, far_a, part_m, near_m, mid_m, far_m,
    x_all, own_sq, got_sq, inv, own, got, hid,
    small_sem, big_sem, out_sem,
    line_s, line_r, owner_s, owner_r,
    na_s, na_r, fa_s, fa_r, nm_s, nm_r, fm_s, fm_r,
    agf_s, agf_r, agn_s, agn_r, sq_s, sq_r, inv_s, inv_r, sum_s, sum_r, hid_s, hid_r,
):
    b, m = lax.axis_index("batch"), lax.axis_index("mp")
    chips = nb // 2
    core, chip = lax.rem(b, 2), lax.div(b, 2)
    mate = b + 1 - 2 * core
    my_slot = core * chips + chip
    length, cols_d = res_buf.shape
    chunks = length // R
    _, _, owners, _, owned = line.shape
    pieces = w_buf.shape[0]
    reuse = sum_r.shape[1]
    units = chunks * pieces
    direct = min(DIRECT, units // (n - 1))
    half = chips * R
    all_rows = nb * R
    heads_here = q_buf.shape[1] // HD
    end = (n - 1) * (1 - core)

    def slot_of(device):
        return lax.rem(device, 2) * chips + lax.div(device, 2)

    kv = lax.div(m * heads_here, HEADS // KV)
    kv = pl.ds(pl.multiple_of(kv * HD, HD), HD)
    small = [
        pltpu.make_async_copy(src, dst, small_sem.at[i])
        for i, (src, dst) in enumerate(
            (
                (q_hbm.at[0], q_buf),
                (k_hbm.at[0, :, kv], k_buf),
                (v_hbm.at[0, :, kv], v_buf),
                (res_hbm.at[0], res_buf),
            )
        )
    ]
    load_wo = pltpu.make_async_copy(wo_hbm, wo_buf, big_sem.at[0])
    load_wd = pltpu.make_async_copy(wd_hbm, wd_buf, big_sem.at[1])

    def piece(c):
        return pl.ds(0, w) if pieces == 1 else pl.ds(pl.multiple_of(c * w, w), w)

    for copy in small:
        copy.start()
    barrier = pltpu.get_barrier_semaphore()
    for axis, at, size in (("mp", m, n), ("batch", b, nb)):
        for k in range(1, size):
            pl.semaphore_signal(
                barrier,
                inc=1,
                device_id={axis: lax.rem(at + k, size)},
                device_id_type=pl.DeviceIdType.MESH,
            )
    load_wo.start()
    for c in range(pieces):
        for i, src in enumerate((wg_hbm, wu_hbm)):
            dst = w_buf.at[c, :, pl.ds(i * w, w)] if joined else w_buf.at[c, i]
            pltpu.make_async_copy(src.at[:, piece(c)], dst, big_sem.at[2]).start()
    load_wd.start()

    at_row = lax.broadcasted_iota(jnp.int32, (R, all_rows), 0)
    at_col = lax.broadcasted_iota(jnp.int32, (R, all_rows), 1)
    for slot in range(nb):
        source = slot_of(perm_ref[2 * (slot % chips) + slot // chips])
        hit = at_col - at_row == source * R
        pmat[slot * R : (slot + 1) * R, :] = jnp.where(hit, 1.0, 0.0).astype(BF16)

    for copy in small[:3]:
        copy.wait()
    q = jnp.concatenate([q_buf[:, h * HD : (h + 1) * HD] for h in range(heads_here)], axis=0)
    scores = lax.dot_general(
        q, k_buf[...], (((1,), (1,)), ((), ())), preferred_element_type=F32
    ) / math.sqrt(HD)
    position = lax.rem(lax.broadcasted_iota(jnp.int32, scores.shape, 0), length)
    causal = position >= lax.broadcasted_iota(jnp.int32, scores.shape, 1)
    scores = jnp.where(causal, scores, -1e30)
    weights = jnp.exp(scores - jnp.max(scores, axis=-1, keepdims=True))
    probability = weights / jnp.sum(weights, axis=-1, keepdims=True)
    mixed = jnp.dot(probability.astype(BF16), v_buf[...], preferred_element_type=F32).astype(BF16)
    for k in range(chunks):
        for h in range(heads_here):
            at = h * HD % owned
            line[m, k, h * HD // owned, :, at : at + HD] = mixed[
                h * length + k * R : h * length + (k + 1) * R
            ]

    def line_copy(source, j, k, peer):
        block = line.at[source, k]
        return remote(block, block, line_s.at[0], line_r.at[k, j - 1], mp=peer)

    def line_send(k):
        for j in range(1, n):
            line_copy(m, j, k, lax.rem(m + j, n)).start()

    def spread_heads(k):
        for j in range(n):
            source = lax.rem(m + n - j, n)
            if j > 0:
                line_copy(source, j, k, source).wait_recv()
            for i in range(owners):
                owner = source * owners + i

                @pl.when(owner != b)
                def _(source=source, i=i, owner=owner):
                    remote(
                        line.at[source, k, i],
                        rows.at[k, my_slot],
                        owner_s.at[k],
                        owner_r.at[k],
                        batch=owner,
                    ).start()

                @pl.when(owner == b)
                def _(source=source, i=i):
                    rows[k, my_slot] = line[source, k, i]

    def all_owners(k):
        block = rows.at[k, pl.ds(0, nb - 1)]
        return remote(block, block, owner_s.at[k], owner_r.at[k], batch=mate)

    scatter_a = (part_a, near_a, mid_a, far_a, na_s, na_r, fa_s, fa_r)
    scatter_m = (part_m, near_m, mid_m, far_m, nm_s, nm_r, fm_s, fm_r)

    part_cols = [pl.ds(h * cols_d // 2, cols_d // 2) for h in range(2)]

    def near_copy(k, h, bufs):
        part, near, mid, far, near_s, near_r, far_s, far_r = bufs
        block = part.at[k, pl.ds((1 - core) * chips, chips), :, part_cols[h]]
        return remote(
            block, near.at[k, :, :, part_cols[h]], near_s.at[0], near_r.at[k, h], batch=mate
        )

    def scatter_far(h, bufs, k):
        part, near, mid, far, near_s, near_r, far_s, far_r = bufs
        near_copy(k, h, bufs).wait_recv()
        at = part_cols[h]
        for j in range(1, chips):
            target = lax.rem(chip + j, chips)
            mid[k, j - 1, :, at] = (
                part[k, core * chips + target, :, at].astype(F32)
                + near[k, target, :, at].astype(F32)
            ).astype(BF16)
            remote(
                mid.at[k, j - 1, :, at],
                far.at[k, j - 1, :, at],
                far_s.at[0],
                far_r.at[k, h],
                batch=2 * target + core,
            ).start()

    def scatter_total(k, h, bufs):
        part, near, mid, far, near_s, near_r, far_s, far_r = bufs
        at = part_cols[h]
        total = part[k, my_slot, :, at].astype(F32) + near[k, chip, :, at].astype(F32)
        remote(
            mid.at[k, :, :, at], far.at[k, :, :, at], far_s.at[0], far_r.at[k, h], batch=mate
        ).wait_recv()
        for j in range(1, chips):
            total = total + far[k, j - 1, :, at].astype(F32)
        return total

    tile = 512 if cols_d % 1024 == 0 else cols_d // 2
    tiles = cols_d // tile // 2

    def multiply_half(k, h, bufs, left, weight):
        for i in range(h * tiles, (h + 1) * tiles):
            at = pl.ds(i * tile, tile)
            made = jnp.dot(left, weight[:, at], preferred_element_type=F32).astype(BF16)
            bufs[0][k, :, :, at] = made.reshape(nb, R, tile)
        near_copy(k, h, bufs).start()

    def swap(k):
        all_owners(k).wait_recv()

        @pl.when(k == 0)
        def _():
            load_wo.wait()

        x = rows[k].reshape(all_rows, owned)
        other = jnp.dot(pmat[...], x, preferred_element_type=F32)
        head = lax.broadcasted_iota(jnp.int32, (all_rows, owned), 1) // HD + b * (owned // HD)
        chosen = head == ablated_ref[0]
        for i in range(1, ablated_ref.shape[0]):
            chosen = chosen | (head == ablated_ref[i])
        swapped[...] = jnp.where(chosen, other, x.astype(F32)).astype(BF16)

    def project(h, k):
        multiply_half(k, h, scatter_a, swapped[...], wo_buf)

    def rows_at(k):
        return pl.ds(pl.multiple_of(k * R, R), R)

    def out_copy(buf, hbm, k, which):
        return pltpu.make_async_copy(
            buf.at[rows_at(k), :], hbm.at[0, rows_at(k), :], out_sem.at[which]
        )

    def gather_far(k, h, j, source, peer):
        block = x_all.at[k, core * chips + source, :, part_cols[h]]
        return remote(block, block, agf_s.at[0], agf_r.at[k, j - 1, h], batch=peer)

    def gather_near(k, h, slots):
        block = x_all.at[k, slots, :, part_cols[h]]
        return remote(block, block, agn_s.at[0], agn_r.at[k, h], batch=mate)

    def square_copy(k):
        place = lax.rem(m + n - end, n) - 1
        return remote(own_sq.at[k], got_sq.at[k, place], sq_s.at[0], sq_r.at[k], mp=end)

    def inverse_wait(k, count):
        block = inv.at[pl.ds(0, count)]
        return remote(block, block, inv_s.at[k], inv_r.at[k], batch=mate)

    def normalize(h, k):
        at = part_cols[h]
        total = scatter_total(k, h, scatter_a)
        attn_buf[rows_at(k), at] = total.astype(BF16)
        state = res_buf[rows_at(k), at].astype(F32) + total
        x_all[k, my_slot, :, at] = (state * gain_ref[at].reshape(1, cols_d // 2)).astype(BF16)
        for j in range(1, chips):
            gather_far(k, h, j, chip, 2 * lax.rem(chip + j, chips) + core).start()
        gather_near(k, h, my_slot).start()
        squares = jnp.broadcast_to(jnp.sum(state * state, axis=1, keepdims=True), (R, 128))
        if h == 0:
            own_sq[k] = squares
            return
        own_sq[k] = own_sq[k] + squares
        out_copy(attn_buf, attn_hbm, k, 0).start()

        @pl.when(m != end)
        def _():
            square_copy(k).start()

    def gather_rest(h, k):
        for j in range(1, chips):
            source = lax.rem(chip + chips - j, chips)
            gather_far(k, h, j, source, mate).wait_recv()
            gather_near(k, h, core * chips + source).start()
        if h == 0:
            return

        @pl.when(m == end)
        def _():
            total = own_sq[k]
            remote(got_sq.at[k], got_sq.at[k], sq_s.at[0], sq_r.at[k], mp=end).wait_recv()
            for j in range(1, n):
                total = total + got_sq[k, j - 1]
            mine = k * chips + chip
            inv[mine] = lax.rsqrt(total / D + 1e-05)
            for j in range(1, nb):
                remote(
                    inv.at[mine],
                    inv.at[mine],
                    inv_s.at[k],
                    inv_r.at[k],
                    batch=lax.rem(b + j, nb),
                ).start()

    pos_of = (m, n - 1 - m)
    way_of = (1, -1)

    def sum_copy(d, u, peer):
        at = lax.rem(u, reuse)
        return remote(own.at[d, u], got.at[d, u], sum_s.at[d], sum_r.at[d, at], mp=peer)

    def hid_copy(d, u, peer):
        block = hid.at[d, u]
        at = lax.rem(u, reuse)
        return remote(block, block, hid_s.at[d], hid_r.at[d, at], mp=peer)

    def hid_direct(d, u, peer):
        block = hid.at[d, u]
        at = lax.rem(u, reuse)
        return remote(block, block, hid_s.at[2 + d], hid_r.at[d, at], mp=peer)

    def cut(offset):
        return lax.div(offset, slots), lax.rem(offset, slots)

    made_cut = cut(jnp.int32(LEAD))
    sum_cut = [cut(LEAD + LAG * pos_of[d]) for d in range(2)]
    back_cut = [cut(LEAD + LAG * (n - 1) + HLAG * (n - 1 - pos_of[d])) for d in range(2)]

    def step(window, s):
        def unit(offset):
            q, r = offset
            late = (s < r).astype(jnp.int32)
            k, c = window - q - late, s - r + slots * late
            return k, c, (k >= 0) & (k < chunks) & (c < pieces)

        k, c, here = unit(made_cut)

        @pl.when(here)
        def _():
            @pl.when(c == 0)
            def _():
                for h in range(2):
                    gather_near(k, h, pl.ds((1 - core) * chips, chips)).wait_recv()

                @pl.when(k == 0)
                def _():
                    pltpu.make_async_copy(w_buf, w_buf, big_sem.at[2]).wait()

            x = x_all[k].reshape(all_rows, cols_d)
            u = k * pieces + c
            if joined:
                made = jnp.dot(x, w_buf[c], preferred_element_type=F32).astype(BF16)
                for d in range(2):
                    own[d, u] = made[d * half : (d + 1) * half]
            else:
                for which in range(2):
                    made = jnp.dot(x, w_buf[c, which], preferred_element_type=F32).astype(BF16)
                    for d in range(2):
                        own[d, u, which] = made[d * half : (d + 1) * half]

        for d in range(2):
            pos, way = pos_of[d], way_of[d]
            k, c, here = unit(sum_cut[d])
            u = k * pieces + c

            @pl.when(here & (pos == 0))
            def _(d=d, u=u, way=way):
                sum_copy(d, u, m + way).start()

            @pl.when(here & (pos > 0) & (pos < n - 1))
            def _(d=d, u=u, way=way):
                sum_copy(d, u, m - way).wait_recv()
                own[d, u] = (own[d, u].astype(F32) + got[d, u].astype(F32)).astype(BF16)
                sum_copy(d, u, m + way).start()

            @pl.when(here & (pos == n - 1))
            def _(d=d, k=k, c=c, u=u, way=way):
                @pl.when(c == 0)
                def _():
                    @pl.when(core == d)
                    def _():
                        inverse_wait(k, chips - 1).wait_recv()

                    @pl.when(core != d)
                    def _():
                        inverse_wait(k, chips).wait_recv()

                sum_copy(d, u, m - way).wait_recv()
                inverse = inv[pl.ds(k * chips, chips)].reshape(half, 128)[:, :1]
                summed = own[d, u].astype(F32) + got[d, u].astype(F32)
                gate = (summed[:, :w] if joined else summed[0]) * inverse
                up = (summed[:, w:] if joined else summed[1]) * inverse
                hid[d, u] = (gate / (1.0 + jnp.exp(-gate)) * up).astype(BF16)

                @pl.when(u < units - direct)
                def _():
                    hid_copy(d, u, m - way).start()

                @pl.when(u >= units - direct)
                def _():
                    for j in range(1, n):
                        hid_direct(d, u, m - way * j).start()

            k, c, here = unit(back_cut[d])
            u = k * pieces + c

            @pl.when(here & (pos < n - 1))
            def _(d=d, u=u, way=way, pos=pos):
                hid_copy(d, u, m + way).wait_recv()

                @pl.when((pos > 0) & (u < units - direct))
                def _():
                    hid_copy(d, u, m - way).start()

        def stage(offset, first, do):
            q, r = divmod(LEAD + offset, slots)
            k = window - q

            @pl.when((s == r) & (k >= first) & (k < chunks))
            def _():
                do(k)

        def start_scatter(k):
            scatter_far(1, scatter_a, k)

            @pl.when(k == 0)
            def _():
                for later in range(2, chunks):
                    line_send(later)

        def down(h, k):
            if h == 0:

                @pl.when(k == 0)
                def _():
                    load_wd.wait()

            left = [
                jnp.concatenate([hid[d, k * pieces + c] for c in range(pieces)], axis=1)
                for d in range(2)
            ]
            multiply_half(k, h, scatter_m, jnp.concatenate(left, axis=0), wd_buf)

        def finish_rows(h, k):
            mlp_buf[rows_at(k), part_cols[h]] = scatter_total(k, h, scatter_m).astype(BF16)
            if h == 1:
                out_copy(mlp_buf, mlp_hbm, k, 1).start()

        for h in range(2):
            stage(done + h, 0, functools.partial(down, h))
        for h in range(2):
            stage(done + 2 + h, 0, functools.partial(scatter_far, h, scatter_m))
        for h in range(2):
            stage(done + FINISH - 1 + h, 0, functools.partial(finish_rows, h))
        stage(-LEAD, 0, swap)
        for h in range(2):
            stage(-LEAD + h, 0, functools.partial(project, h))
        stage(-17, 0, functools.partial(scatter_far, 0, scatter_a))
        stage(-16, 0, start_scatter)
        stage(-26, 1, spread_heads)
        for h in range(2):
            stage(-8 + h, 0, functools.partial(normalize, h))
        for h in range(2):
            stage(-2 + h, 0, functools.partial(gather_rest, h))

    done = pieces - 1 + LAG * (n - 1) + HLAG * (n - 1)
    pl.semaphore_wait(barrier, n + nb - 2)
    line_send(0)
    spread_heads(0)
    if chunks > 1:
        line_send(1)
    small[3].wait()
    last = LEAD + (chunks - 1) * slots + done + FINISH + 1

    def window_steps(window, carry):
        def one(s, carry):
            step(window, s)
            return carry

        return lax.fori_loop(0, slots, one, carry)

    lax.fori_loop(0, -(-last // slots), window_steps, 0)

    pltpu.make_async_copy(attn_buf, attn_hbm.at[0], out_sem.at[0]).wait()
    pltpu.make_async_copy(mlp_buf, mlp_hbm.at[0], out_sem.at[1]).wait()
    block = line.at[pl.ds(0, n - 1)]
    remote(block, block, line_s.at[0], line_r.at[0, 0], mp=end).wait_send()
    for k in range(chunks):
        all_owners(k).wait_send()
    for part, near, mid, far, near_s, near_r, far_s, far_r in (scatter_a, scatter_m):
        remote(near, near, near_s.at[0], near_r.at[0, 0], batch=mate).wait_send()
        remote(mid, mid, far_s.at[0], far_r.at[0, 0], batch=mate).wait_send()
    remote(mid_a, mid_a, agf_s.at[0], agf_r.at[0, 0, 0], batch=mate).wait_send()
    remote(near_a, near_a, agn_s.at[0], agn_r.at[0, 0], batch=mate).wait_send()

    @pl.when(m != end)
    def _():
        remote(own_sq, own_sq, sq_s.at[0], sq_r.at[0], mp=end).wait_send()

    @pl.when(m == end)
    def _():
        for k in range(chunks):
            inverse_wait(k, nb - 1).wait_send()

    for d in range(2):
        pos, way = pos_of[d], way_of[d]

        @pl.when(pos < n - 1)
        def _(d=d, way=way):
            remote(own.at[d], got.at[d], sum_s.at[d], sum_r.at[d, 0], mp=m + way).wait_send()

        @pl.when(pos > 0)
        def _(d=d, way=way):
            block = hid.at[d, pl.ds(0, units - direct)]
            remote(block, block, hid_s.at[d], hid_r.at[d, 0], mp=m - way).wait_send()

        if direct:

            @pl.when(pos == n - 1)
            def _(d=d, way=way):
                block = hid.at[d, pl.ds(0, direct * (n - 1))]
                remote(block, block, hid_s.at[2 + d], hid_r.at[d, 0], mp=m - way).wait_send()


def body(
    residual, query_states, key_states, value_states, prompt_perm, ablated_heads, out_weight,
    rms_gain, gate_weight, up_weight, down_weight,
):
    _, length, cols_d = residual.shape
    nb, n = lax.axis_size("batch"), lax.axis_size("mp")
    chips = nb // 2
    chunks = length // R
    owned = out_weight.shape[0]
    columns = query_states.shape[2]
    owners = columns // owned
    width = gate_weight.shape[1]
    joined = width % 128 == 0
    w = 128 if joined else width
    pieces = width // w
    slots = max(pieces, 14)
    units = chunks * pieces
    reuse = min(units, (LAG + HLAG) * (n - 1) + 1)
    half = chips * R
    pair = (half, 2 * w) if joined else (2, half, w)
    vmem = pl.BlockSpec(memory_space=pltpu.VMEM)
    smem = pl.BlockSpec(memory_space=pltpu.SMEM)
    anywhere = pl.BlockSpec(memory_space=pl.ANY)
    dma = pltpu.SemaphoreType.DMA

    def scatter_bufs():
        return [
            pltpu.VMEM((chunks, nb, R, cols_d), BF16),
            pltpu.VMEM((chunks, chips, R, cols_d), BF16),
            pltpu.VMEM((chunks, chips - 1, R, cols_d), BF16),
            pltpu.VMEM((chunks, chips - 1, R, cols_d), BF16),
        ]

    out = jax.ShapeDtypeStruct((1, length, cols_d), BF16)
    attn, mlp = pl.pallas_call(
        functools.partial(layer_kernel, nb, n, slots, w, joined),
        in_specs=[smem, smem] + [anywhere] * 5 + [vmem] + [anywhere] * 3,
        out_specs=[anywhere, anywhere],
        out_shape=[out, out],
        scratch_shapes=[
            pltpu.VMEM((length, cols_d), BF16),
            pltpu.VMEM((length, cols_d), BF16),
            pltpu.VMEM((length, cols_d), BF16),
            pltpu.VMEM((length, columns), BF16),
            pltpu.VMEM((length, HD), BF16),
            pltpu.VMEM((length, HD), BF16),
            pltpu.VMEM((owned, cols_d), BF16),
            pltpu.VMEM((pieces, cols_d, 2 * w) if joined else (pieces, 2, cols_d, w), BF16),
            pltpu.VMEM((width, cols_d), BF16),
            pltpu.VMEM((nb * R, nb * R), BF16),
            pltpu.VMEM((n, chunks, owners, R, owned), BF16),
            pltpu.VMEM((chunks, nb, R, owned), BF16),
            pltpu.VMEM((nb * R, owned), BF16),
            *scatter_bufs(),
            *scatter_bufs(),
            pltpu.VMEM((chunks, nb, R, cols_d), BF16),
            pltpu.VMEM((chunks, R, 128), F32),
            pltpu.VMEM((chunks, n - 1, R, 128), F32),
            pltpu.VMEM((chunks * chips, R, 128), F32),
            pltpu.VMEM((2, units, *pair), BF16),
            pltpu.VMEM((2, units, *pair), BF16),
            pltpu.VMEM((2, units, half, w), BF16),
            dma((4,)),
            dma((3,)),
            dma((2,)),
            dma((1,)),
            dma((chunks, n - 1)),
            dma((chunks,)),
            dma((chunks,)),
            *[dma((1,)), dma((chunks, 2))] * 4,
            dma((1,)),
            dma((chunks, chips - 1, 2)),
            dma((1,)),
            dma((chunks, 2)),
            dma((1,)),
            dma((chunks,)),
            dma((chunks,)),
            dma((chunks,)),
            dma((2,)),
            dma((2, reuse)),
            dma((4,)),
            dma((2, reuse)),
        ],
        compiler_params=pltpu.CompilerParams(
            collective_id=1, has_side_effects=True, vmem_limit_bytes=VMEM
        ),
    )(
        prompt_perm, ablated_heads, residual, query_states, key_states, value_states, out_weight,
        rms_gain, gate_weight, up_weight, down_weight,
    )
    return pl.pallas_call(
        place_kernel,
        in_specs=[anywhere, anywhere],
        out_specs=[anywhere, anywhere],
        out_shape=[out, out],
        scratch_shapes=[pltpu.VMEM(out.shape, BF16), pltpu.VMEM(out.shape, BF16), dma((2, 2, 2))],
    )(attn, mlp)


def place_kernel(attn_ref, mlp_ref, attn_out, mlp_out, attn_buf, mlp_buf, sem):
    rows = attn_ref.shape[1] // 2
    pairs = ((attn_ref, attn_buf, attn_out), (mlp_ref, mlp_buf, mlp_out))
    moves = [(i, j, pl.ds(j * rows, rows)) for j in range(2) for i in range(2)]

    def load(i, j, at):
        src, buf, dst = pairs[i]
        return pltpu.make_async_copy(src.at[:, at], buf.at[:, at], sem.at[0, i, j])

    def store(i, j, at):
        src, buf, dst = pairs[i]
        return pltpu.make_async_copy(buf.at[:, at], dst.at[:, at], sem.at[1, i, j])

    for move in moves:
        load(*move).start()
    for move in moves:
        load(*move).wait()
        store(*move).start()
    for move in moves:
        store(*move).wait()


def solution(mesh):
    placed = (
        P("batch", None, "mp"),
        P("batch", None, "mp"),
        P("batch", None, None),
        P("batch", None, None),
        P(),
        P(),
        P("batch", "mp"),
        P("mp"),
        P("mp", "batch"),
        P("mp", "batch"),
        P("batch", "mp"),
    )
    return jax.shard_map(
        body,
        mesh=mesh,
        in_specs=placed,
        out_specs=(P("batch", None, "mp"), P("batch", None, "mp")),
        check_vma=False,
    )
```

```python
import functools
import math

import jax
import jax.numpy as jnp
from jax import lax
from jax.experimental import pallas as pl
from jax.experimental.pallas import tpu as pltpu
from jax.sharding import PartitionSpec as P

D = 8192
HEADS = 32
KV = 4
HD = 128
R = 16
LAG = 4
HLAG = 4
LEAD = 20
FINISH = 12
DIRECT = 3
VMEM = 60 * 2**20
BF16, F32 = jnp.bfloat16, jnp.float32


def remote(src, dst, send_sem, recv_sem, **peer):
    return pltpu.make_async_remote_copy(
        src_ref=src,
        dst_ref=dst,
        send_sem=send_sem,
        recv_sem=recv_sem,
        device_id=peer,
        device_id_type=pl.DeviceIdType.MESH,
    )


def layer_kernel(
    nb, n, slots, w, joined,
    perm_ref, ablated_ref, res_hbm, q_hbm, k_hbm, v_hbm, wo_hbm, gain_ref, wg_hbm, wu_hbm, wd_hbm,
    attn_hbm, mlp_hbm,
    attn_buf, mlp_buf, res_buf, q_buf, k_buf, v_buf, wo_buf, w_buf, wd_buf,
    pmat, line, rows, swapped,
    part_a, near_a, mid_a, far_a, part_m, near_m, mid_m, far_m,
    x_all, own_sq, got_sq, inv, own, got, hid,
    small_sem, big_sem, out_sem,
    line_s, line_r, owner_s, owner_r,
    na_s, na_r, fa_s, fa_r, nm_s, nm_r, fm_s, fm_r,
    agf_s, agf_r, agn_s, agn_r, sq_s, sq_r, inv_s, inv_r, sum_s, sum_r, hid_s, hid_r,
):
    b, m = lax.axis_index("batch"), lax.axis_index("mp")
    chips = nb // 2
    core, chip = lax.rem(b, 2), lax.div(b, 2)
    mate = b + 1 - 2 * core
    my_slot = core * chips + chip
    length, cols_d = res_buf.shape
    chunks = length // R
    _, _, owners, _, owned = line.shape
    pieces = w_buf.shape[0]
    reuse = hid_r.shape[1]
    units = chunks * pieces
    direct = min(DIRECT, units // (n - 1))
    half = chips * R
    all_rows = nb * R
    heads_here = q_buf.shape[1] // HD
    end = (n - 1) * (1 - core)

    def slot_of(device):
        return lax.rem(device, 2) * chips + lax.div(device, 2)

    kv = lax.div(m * heads_here, HEADS // KV)
    kv = pl.ds(pl.multiple_of(kv * HD, HD), HD)
    small = [
        pltpu.make_async_copy(src, dst, small_sem.at[i])
        for i, (src, dst) in enumerate(
            (
                (q_hbm.at[0], q_buf),
                (k_hbm.at[0, :, kv], k_buf),
                (v_hbm.at[0, :, kv], v_buf),
                (res_hbm.at[0], res_buf),
            )
        )
    ]
    load_wo = pltpu.make_async_copy(wo_hbm, wo_buf, big_sem.at[0])
    load_wd = pltpu.make_async_copy(wd_hbm, wd_buf, big_sem.at[1])

    def piece(c):
        return pl.ds(0, w) if pieces == 1 else pl.ds(pl.multiple_of(c * w, w), w)

    for copy in small:
        copy.start()
    barrier = pltpu.get_barrier_semaphore()
    for axis, at, size in (("mp", m, n), ("batch", b, nb)):
        for k in range(1, size):
            pl.semaphore_signal(
                barrier,
                inc=1,
                device_id={axis: lax.rem(at + k, size)},
                device_id_type=pl.DeviceIdType.MESH,
            )
    load_wo.start()
    for c in range(pieces):
        for i, src in enumerate((wg_hbm, wu_hbm)):
            dst = w_buf.at[c, :, pl.ds(i * w, w)] if joined else w_buf.at[c, i]
            pltpu.make_async_copy(src.at[:, piece(c)], dst, big_sem.at[2]).start()
    load_wd.start()

    at_row = lax.broadcasted_iota(jnp.int32, (R, all_rows), 0)
    at_col = lax.broadcasted_iota(jnp.int32, (R, all_rows), 1)
    for slot in range(nb):
        source = slot_of(perm_ref[2 * (slot % chips) + slot // chips])
        hit = at_col - at_row == source * R
        pmat[slot * R : (slot + 1) * R, :] = jnp.where(hit, 1.0, 0.0).astype(BF16)

    for copy in small[:3]:
        copy.wait()
    q = jnp.concatenate([q_buf[:, h * HD : (h + 1) * HD] for h in range(heads_here)], axis=0)
    scores = lax.dot_general(
        q, k_buf[...], (((1,), (1,)), ((), ())), preferred_element_type=F32
    ) / math.sqrt(HD)
    position = lax.rem(lax.broadcasted_iota(jnp.int32, scores.shape, 0), length)
    causal = position >= lax.broadcasted_iota(jnp.int32, scores.shape, 1)
    scores = jnp.where(causal, scores, -1e30)
    weights = jnp.exp(scores - jnp.max(scores, axis=-1, keepdims=True))
    probability = weights / jnp.sum(weights, axis=-1, keepdims=True)
    mixed = jnp.dot(probability.astype(BF16), v_buf[...], preferred_element_type=F32).astype(BF16)
    for k in range(chunks):
        for h in range(heads_here):
            at = h * HD % owned
            line[m, k, h * HD // owned, :, at : at + HD] = mixed[
                h * length + k * R : h * length + (k + 1) * R
            ]

    def line_copy(source, j, k, peer):
        block = line.at[source, k]
        return remote(block, block, line_s.at[0], line_r.at[k, j - 1], mp=peer)

    def line_send(k):
        for j in range(1, n):
            line_copy(m, j, k, lax.rem(m + j, n)).start()

    def spread_heads(k):
        for j in range(n):
            source = lax.rem(m + n - j, n)
            if j > 0:
                line_copy(source, j, k, source).wait_recv()
            for i in range(owners):
                owner = source * owners + i

                @pl.when(owner != b)
                def _(source=source, i=i, owner=owner):
                    remote(
                        line.at[source, k, i],
                        rows.at[k, my_slot],
                        owner_s.at[k],
                        owner_r.at[k],
                        batch=owner,
                    ).start()

                @pl.when(owner == b)
                def _(source=source, i=i):
                    rows[k, my_slot] = line[source, k, i]

    def all_owners(k):
        block = rows.at[k, pl.ds(0, nb - 1)]
        return remote(block, block, owner_s.at[k], owner_r.at[k], batch=mate)

    scatter_a = (part_a, near_a, mid_a, far_a, na_s, na_r, fa_s, fa_r)
    scatter_m = (part_m, near_m, mid_m, far_m, nm_s, nm_r, fm_s, fm_r)

    part_cols = [pl.ds(h * cols_d // 2, cols_d // 2) for h in range(2)]

    def near_copy(k, h, bufs):
        part, near, mid, far, near_s, near_r, far_s, far_r = bufs
        block = part.at[k, pl.ds((1 - core) * chips, chips), :, part_cols[h]]
        return remote(
            block, near.at[k, :, :, part_cols[h]], near_s.at[0], near_r.at[k, h], batch=mate
        )

    def scatter_far(h, bufs, k):
        part, near, mid, far, near_s, near_r, far_s, far_r = bufs
        near_copy(k, h, bufs).wait_recv()
        at = part_cols[h]
        for j in range(1, chips):
            target = lax.rem(chip + j, chips)
            mid[k, j - 1, :, at] = (
                part[k, core * chips + target, :, at].astype(F32)
                + near[k, target, :, at].astype(F32)
            ).astype(BF16)
            remote(
                mid.at[k, j - 1, :, at],
                far.at[k, j - 1, :, at],
                far_s.at[0],
                far_r.at[k, h],
                batch=2 * target + core,
            ).start()

    def scatter_total(k, h, bufs):
        part, near, mid, far, near_s, near_r, far_s, far_r = bufs
        at = part_cols[h]
        total = part[k, my_slot, :, at].astype(F32) + near[k, chip, :, at].astype(F32)
        remote(
            mid.at[k, :, :, at], far.at[k, :, :, at], far_s.at[0], far_r.at[k, h], batch=mate
        ).wait_recv()
        for j in range(1, chips):
            total = total + far[k, j - 1, :, at].astype(F32)
        return total

    tile = 512 if cols_d % 1024 == 0 else cols_d // 2
    tiles = cols_d // tile // 2

    def multiply_half(k, h, bufs, left, weight):
        for i in range(h * tiles, (h + 1) * tiles):
            at = pl.ds(i * tile, tile)
            made = jnp.dot(left, weight[:, at], preferred_element_type=F32).astype(BF16)
            bufs[0][k, :, :, at] = made.reshape(nb, R, tile)
        near_copy(k, h, bufs).start()

    def swap(k):
        all_owners(k).wait_recv()

        @pl.when(k == 0)
        def _():
            load_wo.wait()

        x = rows[k].reshape(all_rows, owned)
        other = jnp.dot(pmat[...], x, preferred_element_type=F32)
        head = lax.broadcasted_iota(jnp.int32, (all_rows, owned), 1) // HD + b * (owned // HD)
        chosen = head == ablated_ref[0]
        for i in range(1, ablated_ref.shape[0]):
            chosen = chosen | (head == ablated_ref[i])
        swapped[...] = jnp.where(chosen, other, x.astype(F32)).astype(BF16)

    def project(h, k):
        multiply_half(k, h, scatter_a, swapped[...], wo_buf)

    def rows_at(k):
        return pl.ds(pl.multiple_of(k * R, R), R)

    def out_copy(buf, hbm, k, which):
        return pltpu.make_async_copy(
            buf.at[rows_at(k), :], hbm.at[0, rows_at(k), :], out_sem.at[which]
        )

    def gather_far(k, h, j, source, peer):
        block = x_all.at[k, core * chips + source, :, part_cols[h]]
        return remote(block, block, agf_s.at[0], agf_r.at[k, j - 1, h], batch=peer)

    def gather_near(k, h, slots):
        block = x_all.at[k, slots, :, part_cols[h]]
        return remote(block, block, agn_s.at[0], agn_r.at[k, h], batch=mate)

    def square_copy(k):
        place = lax.rem(m + n - end, n) - 1
        return remote(own_sq.at[k], got_sq.at[k, place], sq_s.at[0], sq_r.at[k], mp=end)

    def inverse_wait(k, count):
        block = inv.at[pl.ds(0, count)]
        return remote(block, block, inv_s.at[k], inv_r.at[k], batch=mate)

    def normalize(h, k):
        at = part_cols[h]
        total = scatter_total(k, h, scatter_a)
        attn_buf[rows_at(k), at] = total.astype(BF16)
        state = res_buf[rows_at(k), at].astype(F32) + total
        x_all[k, my_slot, :, at] = (state * gain_ref[at].reshape(1, cols_d // 2)).astype(BF16)
        for j in range(1, chips):
            gather_far(k, h, j, chip, 2 * lax.rem(chip + j, chips) + core).start()
        gather_near(k, h, my_slot).start()
        squares = jnp.broadcast_to(jnp.sum(state * state, axis=1, keepdims=True), (R, 128))
        if h == 0:
            own_sq[k] = squares
            return
        own_sq[k] = own_sq[k] + squares
        out_copy(attn_buf, attn_hbm, k, 0).start()

        @pl.when(m != end)
        def _():
            square_copy(k).start()

    def gather_rest(h, k):
        for j in range(1, chips):
            source = lax.rem(chip + chips - j, chips)
            gather_far(k, h, j, source, mate).wait_recv()
            gather_near(k, h, core * chips + source).start()
        if h == 0:
            return

        @pl.when(m == end)
        def _():
            total = own_sq[k]
            remote(got_sq.at[k], got_sq.at[k], sq_s.at[0], sq_r.at[k], mp=end).wait_recv()
            for j in range(1, n):
                total = total + got_sq[k, j - 1]
            mine = k * chips + chip
            inv[mine] = lax.rsqrt(total / D + 1e-05)
            for j in range(1, nb):
                remote(
                    inv.at[mine],
                    inv.at[mine],
                    inv_s.at[k],
                    inv_r.at[k],
                    batch=lax.rem(b + j, nb),
                ).start()

    pos_of = (m, n - 1 - m)
    way_of = (1, -1)

    def sum_copy(d, u, peer):
        at = lax.rem(u, sum_r.shape[1])
        return remote(own.at[d, u], got.at[d, u], sum_s.at[d], sum_r.at[d, at], mp=peer)

    def hid_copy(d, u, peer):
        block = hid.at[d, u]
        at = lax.rem(u, reuse)
        return remote(block, block, hid_s.at[d], hid_r.at[d, at], mp=peer)

    def hid_direct(d, u, peer):
        block = hid.at[d, u]
        at = lax.rem(u, reuse)
        return remote(block, block, hid_s.at[2 + d], hid_r.at[d, at], mp=peer)

    def cut(offset):
        return lax.div(offset, slots), lax.rem(offset, slots)

    made_cut = cut(jnp.int32(LEAD))
    sum_cut = [cut(LEAD + LAG * pos_of[d]) for d in range(2)]
    back_cut = [cut(LEAD + LAG * (n - 1) + HLAG * (n - 1 - pos_of[d])) for d in range(2)]

    def step(window, s):
        def unit(offset):
            q, r = offset
            late = (s < r).astype(jnp.int32)
            k, c = window - q - late, s - r + slots * late
            return k, c, (k >= 0) & (k < chunks) & (c < pieces)

        k, c, here = unit(made_cut)

        @pl.when(here)
        def _():
            @pl.when(c == 0)
            def _():
                for h in range(2):
                    gather_near(k, h, pl.ds((1 - core) * chips, chips)).wait_recv()

                @pl.when(k == 0)
                def _():
                    pltpu.make_async_copy(w_buf, w_buf, big_sem.at[2]).wait()

            x = x_all[k].reshape(all_rows, cols_d)
            u = k * pieces + c
            if joined:
                made = jnp.dot(x, w_buf[c], preferred_element_type=F32).astype(BF16)
                for d in range(2):
                    own[d, u] = made[d * half : (d + 1) * half]
            else:
                for which in range(2):
                    made = jnp.dot(x, w_buf[c, which], preferred_element_type=F32).astype(BF16)
                    for d in range(2):
                        own[d, u, which] = made[d * half : (d + 1) * half]

        for d in range(2):
            pos, way = pos_of[d], way_of[d]
            k, c, here = unit(sum_cut[d])
            u = k * pieces + c

            @pl.when(here & (pos == 0))
            def _(d=d, u=u, way=way):
                sum_copy(d, u, m + way).start()

            @pl.when(here & (pos > 0) & (pos < n - 1))
            def _(d=d, u=u, way=way):
                sum_copy(d, u, m - way).wait_recv()
                own[d, u] = (own[d, u].astype(F32) + got[d, u].astype(F32)).astype(BF16)
                sum_copy(d, u, m + way).start()

            @pl.when(here & (pos == n - 1))
            def _(d=d, k=k, c=c, u=u, way=way):
                @pl.when(c == 0)
                def _():
                    @pl.when(core == d)
                    def _():
                        inverse_wait(k, chips - 1).wait_recv()

                    @pl.when(core != d)
                    def _():
                        inverse_wait(k, chips).wait_recv()

                sum_copy(d, u, m - way).wait_recv()
                inverse = inv[pl.ds(k * chips, chips)].reshape(half, 128)[:, :1]
                summed = own[d, u].astype(F32) + got[d, u].astype(F32)
                gate = (summed[:, :w] if joined else summed[0]) * inverse
                up = (summed[:, w:] if joined else summed[1]) * inverse
                hid[d, u] = (gate / (1.0 + jnp.exp(-gate)) * up).astype(BF16)

                @pl.when(u < units - direct)
                def _():
                    hid_copy(d, u, m - way).start()

                @pl.when(u >= units - direct)
                def _():
                    for j in range(1, n):
                        hid_direct(d, u, m - way * j).start()

            k, c, here = unit(back_cut[d])
            u = k * pieces + c

            @pl.when(here & (pos < n - 1))
            def _(d=d, u=u, way=way, pos=pos):
                hid_copy(d, u, m + way).wait_recv()

                @pl.when((pos > 0) & (u < units - direct))
                def _():
                    hid_copy(d, u, m - way).start()

        def stage(offset, first, do):
            q, r = divmod(LEAD + offset, slots)
            k = window - q

            @pl.when((s == r) & (k >= first) & (k < chunks))
            def _():
                do(k)

        def start_scatter(k):
            scatter_far(1, scatter_a, k)

            @pl.when(k == 0)
            def _():
                for later in range(2, chunks):
                    line_send(later)

        def down(h, k):
            if h == 0:

                @pl.when(k == 0)
                def _():
                    load_wd.wait()

            left = [
                jnp.concatenate([hid[d, k * pieces + c] for c in range(pieces)], axis=1)
                for d in range(2)
            ]
            multiply_half(k, h, scatter_m, jnp.concatenate(left, axis=0), wd_buf)

        def finish_rows(h, k):
            mlp_buf[rows_at(k), part_cols[h]] = scatter_total(k, h, scatter_m).astype(BF16)
            if h == 1:
                out_copy(mlp_buf, mlp_hbm, k, 1).start()

        for h in range(2):
            stage(done + h, 0, functools.partial(down, h))
        for h in range(2):
            stage(done + 2 + h, 0, functools.partial(scatter_far, h, scatter_m))
        for h in range(2):
            stage(done + FINISH - 1 + h, 0, functools.partial(finish_rows, h))
        stage(-LEAD, 0, swap)
        for h in range(2):
            stage(-LEAD + h, 0, functools.partial(project, h))
        stage(-17, 0, functools.partial(scatter_far, 0, scatter_a))
        stage(-16, 0, start_scatter)
        stage(-26, 1, spread_heads)
        for h in range(2):
            stage(-8 + h, 0, functools.partial(normalize, h))
        for h in range(2):
            stage(-2 + h, 0, functools.partial(gather_rest, h))

    done = pieces - 1 + LAG * (n - 1) + HLAG * (n - 1)
    pl.semaphore_wait(barrier, n + nb - 2)
    line_send(0)
    spread_heads(0)
    if chunks > 1:
        line_send(1)
    small[3].wait()
    last = LEAD + (chunks - 1) * slots + done + FINISH + 1

    def window_steps(window, carry):
        def one(s, carry):
            step(window, s)
            return carry

        return lax.fori_loop(0, slots, one, carry)

    lax.fori_loop(0, -(-last // slots), window_steps, 0)

    pltpu.make_async_copy(attn_buf, attn_hbm.at[0], out_sem.at[0]).wait()
    pltpu.make_async_copy(mlp_buf, mlp_hbm.at[0], out_sem.at[1]).wait()
    block = line.at[pl.ds(0, n - 1)]
    remote(block, block, line_s.at[0], line_r.at[0, 0], mp=end).wait_send()
    for k in range(chunks):
        all_owners(k).wait_send()
    for part, near, mid, far, near_s, near_r, far_s, far_r in (scatter_a, scatter_m):
        remote(near, near, near_s.at[0], near_r.at[0, 0], batch=mate).wait_send()
        remote(mid, mid, far_s.at[0], far_r.at[0, 0], batch=mate).wait_send()
    remote(mid_a, mid_a, agf_s.at[0], agf_r.at[0, 0, 0], batch=mate).wait_send()
    remote(near_a, near_a, agn_s.at[0], agn_r.at[0, 0], batch=mate).wait_send()

    @pl.when(m != end)
    def _():
        remote(own_sq, own_sq, sq_s.at[0], sq_r.at[0], mp=end).wait_send()

    @pl.when(m == end)
    def _():
        for k in range(chunks):
            inverse_wait(k, nb - 1).wait_send()

    for d in range(2):
        pos, way = pos_of[d], way_of[d]

        @pl.when(pos < n - 1)
        def _(d=d, way=way):
            remote(own.at[d], got.at[d], sum_s.at[d], sum_r.at[d, 0], mp=m + way).wait_send()

        @pl.when(pos > 0)
        def _(d=d, way=way):
            block = hid.at[d, pl.ds(0, units - direct)]
            remote(block, block, hid_s.at[d], hid_r.at[d, 0], mp=m - way).wait_send()

        if direct:

            @pl.when(pos == n - 1)
            def _(d=d, way=way):
                block = hid.at[d, pl.ds(0, direct * (n - 1))]
                remote(block, block, hid_s.at[2 + d], hid_r.at[d, 0], mp=m - way).wait_send()


def body(
    residual, query_states, key_states, value_states, prompt_perm, ablated_heads, out_weight,
    rms_gain, gate_weight, up_weight, down_weight,
):
    _, length, cols_d = residual.shape
    nb, n = lax.axis_size("batch"), lax.axis_size("mp")
    chips = nb // 2
    chunks = length // R
    owned = out_weight.shape[0]
    columns = query_states.shape[2]
    owners = columns // owned
    width = gate_weight.shape[1]
    joined = width % 128 == 0
    w = 128 if joined else width
    pieces = width // w
    slots = max(pieces, 14)
    units = chunks * pieces
    reuse = min(units, (LAG + HLAG) * (n - 1) + 1)
    half = chips * R
    pair = (half, 2 * w) if joined else (2, half, w)
    vmem = pl.BlockSpec(memory_space=pltpu.VMEM)
    smem = pl.BlockSpec(memory_space=pltpu.SMEM)
    anywhere = pl.BlockSpec(memory_space=pl.ANY)
    dma = pltpu.SemaphoreType.DMA

    def scatter_bufs():
        return [
            pltpu.VMEM((chunks, nb, R, cols_d), BF16),
            pltpu.VMEM((chunks, chips, R, cols_d), BF16),
            pltpu.VMEM((chunks, chips - 1, R, cols_d), BF16),
            pltpu.VMEM((chunks, chips - 1, R, cols_d), BF16),
        ]

    out = jax.ShapeDtypeStruct((1, length, cols_d), BF16)
    attn, mlp = pl.pallas_call(
        functools.partial(layer_kernel, nb, n, slots, w, joined),
        in_specs=[smem, smem] + [anywhere] * 5 + [vmem] + [anywhere] * 3,
        out_specs=[anywhere, anywhere],
        out_shape=[out, out],
        scratch_shapes=[
            pltpu.VMEM((length, cols_d), BF16),
            pltpu.VMEM((length, cols_d), BF16),
            pltpu.VMEM((length, cols_d), BF16),
            pltpu.VMEM((length, columns), BF16),
            pltpu.VMEM((length, HD), BF16),
            pltpu.VMEM((length, HD), BF16),
            pltpu.VMEM((owned, cols_d), BF16),
            pltpu.VMEM((pieces, cols_d, 2 * w) if joined else (pieces, 2, cols_d, w), BF16),
            pltpu.VMEM((width, cols_d), BF16),
            pltpu.VMEM((nb * R, nb * R), BF16),
            pltpu.VMEM((n, chunks, owners, R, owned), BF16),
            pltpu.VMEM((chunks, nb, R, owned), BF16),
            pltpu.VMEM((nb * R, owned), BF16),
            *scatter_bufs(),
            *scatter_bufs(),
            pltpu.VMEM((chunks, nb, R, cols_d), BF16),
            pltpu.VMEM((chunks, R, 128), F32),
            pltpu.VMEM((chunks, n - 1, R, 128), F32),
            pltpu.VMEM((chunks * chips, R, 128), F32),
            pltpu.VMEM((2, units, *pair), BF16),
            pltpu.VMEM((2, units, *pair), BF16),
            pltpu.VMEM((2, units, half, w), BF16),
            dma((4,)),
            dma((3,)),
            dma((2,)),
            dma((1,)),
            dma((chunks, n - 1)),
            dma((chunks,)),
            dma((chunks,)),
            *[dma((1,)), dma((chunks, 2))] * 4,
            dma((1,)),
            dma((chunks, chips - 1, 2)),
            dma((1,)),
            dma((chunks, 2)),
            dma((1,)),
            dma((chunks,)),
            dma((chunks,)),
            dma((chunks,)),
            dma((2,)),
            dma((2, min(units, LAG * (n - 1) + 2))),
            dma((4,)),
            dma((2, reuse)),
        ],
        compiler_params=pltpu.CompilerParams(
            collective_id=1, has_side_effects=True, vmem_limit_bytes=VMEM
        ),
    )(
        prompt_perm, ablated_heads, residual, query_states, key_states, value_states, out_weight,
        rms_gain, gate_weight, up_weight, down_weight,
    )
    return pl.pallas_call(
        place_kernel,
        in_specs=[anywhere, anywhere],
        out_specs=[anywhere, anywhere],
        out_shape=[out, out],
        scratch_shapes=[pltpu.VMEM(out.shape, BF16), pltpu.VMEM(out.shape, BF16), dma((2, 2, 4))],
    )(attn, mlp)


def place_kernel(attn_ref, mlp_ref, attn_out, mlp_out, attn_buf, mlp_buf, sem):
    rows = attn_ref.shape[1] // 4
    pairs = ((attn_ref, attn_buf, attn_out), (mlp_ref, mlp_buf, mlp_out))
    moves = [(i, j, pl.ds(j * rows, rows)) for j in range(4) for i in range(2)]

    def load(i, j, at):
        src, buf, dst = pairs[i]
        return pltpu.make_async_copy(src.at[:, at], buf.at[:, at], sem.at[0, i, j])

    def store(i, j, at):
        src, buf, dst = pairs[i]
        return pltpu.make_async_copy(buf.at[:, at], dst.at[:, at], sem.at[1, i, j])

    for move in moves:
        load(*move).start()
    for move in moves:
        load(*move).wait()
        store(*move).start()
    for move in moves:
        store(*move).wait()


def solution(mesh):
    placed = (
        P("batch", None, "mp"),
        P("batch", None, "mp"),
        P("batch", None, None),
        P("batch", None, None),
        P(),
        P(),
        P("batch", "mp"),
        P("mp"),
        P("mp", "batch"),
        P("mp", "batch"),
        P("batch", "mp"),
    )
    return jax.shard_map(
        body,
        mesh=mesh,
        in_specs=placed,
        out_specs=(P("batch", None, "mp"), P("batch", None, "mp")),
        check_vma=False,
    )
```
